32 devices in a mesh: grp: 1, ep: 16 (over z, y, core), tp: 2 (over x).
Axes of the slice: x: 2, y: 2, z: 4, core: 2. Of those that a mesh axis runs over, the one named last changes fastest.
Arguments:
- tokens: bfloat16 [2560, 3072], P(('grp', 'ep'), 'tp'), may hold values from -6 to 6
- expert_ids: int32 [2560, 12], P(('grp', 'ep')), may hold values from 0 to 23, all different within a row; in each aligned block of 160 rows (0 to 159, 160 to 319, ...) at most 120 rows name the same one
- gate_weights: float32 [2560, 12], P(('grp', 'ep')), may hold values from 0.02 to 0.2
- expert_hidden: bfloat16 [16, 1920, 1024], P('ep', ('grp', 'tp')), may hold values from -6 to 6
- expert_down: bfloat16 [16, 1024, 3072], P('ep', None, 'tp'), may hold values from -0.1875 to 0.1875
- dense_hidden: bfloat16 [2560, 6144], P(('grp', 'ep'), 'tp'), may hold values from -6 to 6
- dense_down: bfloat16 [6144, 3072], P('tp', 'ep'), may hold values from -0.078125 to 0.078125
Outputs:
- mixed: bfloat16 [2560, 3072], P(('grp', 'ep'), 'tp')
The draws below stay inside these ranges and needn't reach their ends.
Inputs may be any that keep to these rules, and one draw needn't show every extreme that they name: `expert_ids`: each row names 12 different ids; ids below 16 are experts with weights, the others zero experts. In each aligned block of 160 rows no id is named by more than 120 rows, a bound that some block reaches.
All inputs are finite; a program needn't handle non-finite values.
Results may differ from the reference program's by a relative error of at most 0.0038.
Values may be sent and summed in bfloat16 or wider, within the bound.
No kernel may reach another device: no remote copies, remote signals or barrier semaphores. Data moves between devices by JAX's collectives and lax.ppermute only.
A program may use at most 128 MiB of HBM per device.

```python
import math
import jax
import jax.numpy as jnp
import numpy as np
from jax import lax

D = 3072
EH = 1024
FF = 6144
TOP = 12
TOK_DEV = 160
EXPERTS = 16
ZEROS = 8
CAP = 120
SLOTS = 1920
TOKENS = 2560
N_EP = 16


def levels(key, dims, cuts, low, top_value):
    def one(dim, shards_of):
        heights = jax.random.uniform(jax.random.fold_in(jax.random.fold_in(key, 6), dim), (shards_of,), jnp.float32, low / len(cuts), top_value / len(cuts))
        return jnp.repeat(jnp.exp(heights), dims[dim] // shards_of).reshape((-1,) + (1,) * (len(dims) - dim - 1))

    factor_of = one(*cuts[0])
    for cut in cuts[1:]:
        factor_of = factor_of * one(*cut)
    return factor_of


def assign_block(key, own, number, rows, amount, top, reach, lean):
    ranking = jax.random.permutation(key, amount)
    heavy_load, ordinary = shares(amount, rows * top, reach, lean, True), shares(amount, rows * top, reach, lean, False)
    places = jnp.arange(amount)

    def named(lengths, turn):
        used = int((lengths > 0).sum())
        fixed = max(1, used // 4)
        moved = fixed + (places - fixed + turn * (used - fixed)) % max(1, amount - fixed)
        return jnp.zeros((amount,), jnp.int32).at[ranking[jnp.where(places < fixed, places, moved)]].set(jnp.asarray(lengths, jnp.int32))

    lengths = jnp.where(number % 4 == 0, named(heavy_load, number // 4), named(ordinary, number - number // 4 - 1))
    mixed = jax.random.permutation(jax.random.fold_in(own, 3), amount)
    source_of, receiver = mixed[0:amount // 2 * 2:2], mixed[1:amount // 2 * 2:2]
    slack = jnp.minimum(lengths[source_of] - 1, reach - lengths[receiver]) // 2
    slack = jnp.where((source_of == ranking[0]) | (receiver == ranking[0]) | (lengths[receiver] == 0), 0, jnp.maximum(slack, 0))
    moved = jax.random.randint(jax.random.fold_in(own, 4), (amount // 2,), 0, 1 << 20) % (slack + 1)
    lengths = lengths.at[source_of].add(-moved).at[receiver].add(moved)
    items = jnp.searchsorted(jnp.cumsum(lengths), jnp.arange(rows * top), side="right").astype(jnp.int32)
    table = items.reshape(top, rows).T
    table = table[jax.random.permutation(jax.random.fold_in(own, 1), rows)]
    turn = jax.random.randint(jax.random.fold_in(own, 2), (rows, 1), 0, top)
    return jnp.take_along_axis(table, (jnp.arange(top)[None, :] + turn) % top, axis=1)


def shares(amount, total, limit, slope, full):
    portions = [(1 << 20) // math.isqrt(rank ** slope) + 1 for rank in range(1, amount + 1)]
    largest = limit if full else min(limit, max(-(-total // amount), total * portions[0] // sum(portions)))
    least = 1 if total - largest >= amount - 1 else 0
    counts, spare = [largest] + [least] * (amount - 1), total - largest - least * (amount - 1)
    while spare > 0:
        candidates = [i for i in range(1, amount) if counts[i] < largest] or [i for i in range(1, amount) if counts[i] < limit]
        mass, left = sum([portions[i] for i in candidates]), spare
        for i in candidates:
            more = min(limit - counts[i], max(1, left * portions[i] // mass), spare)
            counts[i] = counts[i] + more
            spare = spare - more
    return np.array(counts)


def centred(own_key, dims, deviation, reach, split=(), held_as=jnp.bfloat16):
    drawn = jax.random.normal(own_key, dims, jnp.float32) * deviation
    if len(split) > 0:
        drawn = levels(own_key, dims, split, -0.22, 0.18) * drawn
    return jnp.clip(drawn, min=-reach, max=reach).astype(held_as)


def setup_inputs(seed: int = 0, part: int = 0) -> dict:
    splits = jax.random.split(jax.random.key(seed), 8)
    part_splits = jax.random.split(jax.random.fold_in(splits[7], part), 8)
    tokens = centred(part_splits[0], (TOKENS, D), 1.0, 6.0, ((0, 16), (1, 2)))
    expert_ids_keys = jax.random.split(jax.random.fold_in(part_splits[1], 1), TOKENS // TOK_DEV)
    expert_ids_turns = jax.random.permutation(jax.random.fold_in(part_splits[1], 3), TOKENS // TOK_DEV)
    expert_ids = jax.vmap(lambda own, number: assign_block(jax.random.fold_in(part_splits[1], 2), own, number, TOK_DEV, EXPERTS + ZEROS, TOP, CAP, 2))(expert_ids_keys, expert_ids_turns).reshape((TOKENS, TOP))
    gate_weights = jnp.clip(0.02 + 0.18 * jax.random.uniform(part_splits[2], (TOKENS, TOP), jnp.float32) ** levels(part_splits[2], (TOKENS, TOP), ((0, 16),), -0.2, 0.2), 0.02, 0.2)
    expert_hidden = centred(part_splits[3], (EXPERTS, SLOTS, EH), 1.0, 6.0, ((0, 16), (1, 2)))
    expert_down = centred(splits[4], (EXPERTS, EH, D), EH ** -0.5, 0.1875, ((0, 16), (2, 2)))
    dense_hidden = centred(part_splits[5], (TOKENS, FF), 1.0, 6.0, ((0, 16), (1, 2)))
    dense_down = centred(splits[6], (FF, D), FF ** -0.5, 0.078125, ((0, 2), (1, 16)))
    return dict(tokens=tokens, expert_ids=expert_ids, gate_weights=gate_weights, expert_hidden=expert_hidden, expert_down=expert_down, dense_hidden=dense_hidden, dense_down=dense_down)


def slot_numbers(block_ids):
    flat = block_ids.reshape(-1)
    kinds = jnp.arange(EXPERTS + ZEROS, dtype=jnp.int32)
    marks = (flat[:, None] == kinds[None, :]).astype(jnp.int32)
    before = jnp.cumsum(marks, axis=0) - marks
    return jnp.sum(before * marks, axis=1).astype(jnp.int32).reshape(block_ids.shape)


def reference(tokens, expert_ids, gate_weights, expert_hidden, expert_down, dense_hidden, dense_down):
    blocks = expert_ids.reshape(N_EP, TOK_DEV, TOP)
    slots = jax.vmap(slot_numbers)(blocks).reshape(TOKENS, TOP)
    genuine = expert_ids < EXPERTS
    owner = (jnp.arange(TOKENS, dtype=jnp.int32) // TOK_DEV).astype(jnp.int32)[:, None]
    position = (owner * CAP + slots).astype(jnp.int32)
    target = jnp.where(genuine, expert_ids, EXPERTS).astype(jnp.int32)
    token_index = jnp.broadcast_to(jnp.arange(TOKENS, dtype=jnp.int32)[:, None], (TOKENS, TOP))
    slot_token = jnp.zeros((EXPERTS, SLOTS), jnp.int32).at[target, position].set(token_index, mode="drop")
    slot_gate = jnp.zeros((EXPERTS, SLOTS), jnp.float32).at[target, position].set(gate_weights, mode="drop")

    def add_expert(total, pieces):
        hidden, down, where_to, weight = pieces
        rounded = jnp.dot(hidden, down, preferred_element_type=jnp.float32).astype(jnp.bfloat16)
        rounded = lax.optimization_barrier(rounded)
        return total.at[where_to].add(weight[:, None] * rounded.astype(jnp.float32)), None

    routed, _ = lax.scan(add_expert, jnp.zeros((TOKENS, D), jnp.float32),
                         (expert_hidden, expert_down, slot_token, slot_gate))
    zero_gate = jnp.sum(jnp.where(genuine, jnp.float32(0.0), gate_weights), axis=1)
    identity = zero_gate[:, None] * tokens.astype(jnp.float32)
    dense = jnp.dot(dense_hidden, dense_down, preferred_element_type=jnp.float32)
    return (dense + routed + identity).astype(jnp.bfloat16)
```

```python
import jax
import jax.numpy as jnp
from jax import lax
from jax.sharding import Mesh, PartitionSpec as P

F32 = jnp.float32
BF16 = jnp.bfloat16
SWAP = ((0, 1), (1, 0))


def pick(array, index, axis=0):
    return lax.dynamic_index_in_dim(array, index, axis, keepdims=False)


def gate_rows(expert_ids, gate_weights, experts):
    ids, gates = expert_ids.T, gate_weights.T
    labels = jnp.arange(experts, dtype=jnp.int32)[:, None, None]
    return jnp.max(jnp.where(ids[None] == labels, gates[None], F32(-1.0)), axis=1)


def spread_gates(rows, zs, y, z):
    c = lax.axis_index("c")
    rows = rows.reshape(zs, 2, 2, rows.shape[-1])
    mine = pick(rows, y, 1)
    other = lax.ppermute(pick(rows, 1 - y, 1), "y", SWAP)
    both = jnp.stack([jnp.where(y == 0, mine, other), jnp.where(y == 0, other, mine)], 1)
    both = jnp.stack([pick(both, c, 2), pick(both, 1 - c, 2)], 2)
    got = [pick(both, z)]
    for shift in range(1, zs):
        got.append(lax.ppermute(pick(both, (z + shift) % zs), "z", [(i, (i + shift) % zs) for i in range(zs)]))
    got = jnp.stack(got)
    return jnp.stack([pick(got, (z - i) % zs) for i in range(zs)])


def placement(gates, capacity):
    tokens = gates.shape[-1]
    picked = gates >= 0
    order = jnp.arange(tokens)
    earlier = (order[:, None] < order[None, :]).astype(BF16)
    slots = jnp.dot(picked.astype(BF16), earlier, preferred_element_type=F32).astype(jnp.int32)
    slots = jnp.where(picked, slots, -1)
    places = jnp.arange(capacity, dtype=jnp.int32)
    table = jnp.where(slots[..., None] == places, gates[..., None], F32(0.0))
    table = jnp.moveaxis(table, -3, -2)
    table = table.reshape(table.shape[:-2] + (2 * capacity,))
    high = table.astype(BF16)
    low = (table - high.astype(F32)).astype(BF16)
    return high, low


def local(tokens, expert_ids, gate_weights, expert_hidden, expert_down, dense_hidden, dense_down):
    zs, tp = lax.axis_size("z"), lax.axis_size("tp")
    z, y, c, x = (lax.axis_index(name) for name in ("z", "y", "c", "tp"))
    experts = zs * 4
    zt = zs // tp
    rows = tokens.shape[0]
    hidden, down = expert_hidden[0], expert_down[0]
    capacity = hidden.shape[0] // (zt * 4)
    features = down.shape[1]

    hidden = hidden.reshape(zt, 4 * capacity, hidden.shape[1])

    def turn(owner, k):
        return jnp.where(2 * owner < tp, k, zt - 1 - k)

    def turn_of(owner, k):
        return k if 2 * owner < tp else zt - 1 - k

    chunks = []
    for k in range(zt):
        chunks.append((0, k, pick(hidden, turn(x, k))))
    for shift in range(1, tp):
        for k in range(zt):
            sent = chunks[k][2]
            moved = lax.ppermute(sent, "tp", [((i + shift) % tp, i) for i in range(tp)])
            chunks.append((shift, k, moved))

    right = [(i, i + 1) for i in range(zs - 1)]
    left = [(i + 1, i) for i in range(zs - 1)]
    acts = jnp.stack([dense_hidden, lax.ppermute(dense_hidden, "y", SWAP)])
    acts = acts.reshape(2 * rows, -1)
    columns = dense_down.shape[1]

    def product(weights):
        sibling = lax.ppermute(weights, "c", SWAP)
        first = jnp.where(c == 0, weights, sibling)
        second = jnp.where(c == 0, sibling, weights)
        both = jnp.concatenate([first, second], 1)
        return jnp.dot(acts, both, preferred_element_type=F32).astype(BF16)

    sheet = jnp.zeros((zs, 2 * rows, 2 * columns), BF16)
    if zs <= 4:
        sheet = lax.dynamic_update_index_in_dim(sheet, product(dense_down), z, 0)
        from_left = from_right = dense_down
        for step in range(1, zs):
            from_left = lax.ppermute(from_left, "z", right)
            from_right = lax.ppermute(from_right, "z", left)
            for value, at in ((from_left, z - step), (from_right, z + step)):
                inside = (at >= 0) & (at < zs)
                at = jnp.clip(at, 0, zs - 1)
                value = jnp.where(inside, product(value), pick(sheet, at))
                sheet = lax.dynamic_update_index_in_dim(sheet, value, at, 0)
    else:
        every = lax.all_gather(dense_down, "z")
        for i in range(zs):
            sheet = lax.dynamic_update_index_in_dim(sheet, product(every[i]), i, 0)

    gates = spread_gates(gate_rows(expert_ids, gate_weights, experts), zs, y, z)
    high, low = placement(gates, capacity)

    def partial_sum(chunk, at):
        out = jnp.dot(chunk, down, preferred_element_type=F32).astype(BF16)
        out = out.reshape(2, 2, capacity, features)
        sibling = lax.ppermute(pick(out, 1 - c, 1), "c", SWAP)
        table = jnp.concatenate([pick(out, c, 1), sibling], 1)
        p_high, p_low = pick(high, at), pick(low, at)

        def combined(which):
            t = pick(table, which)
            return jnp.dot(pick(p_high, which), t, preferred_element_type=F32) + jnp.dot(
                pick(p_low, which), t, preferred_element_type=F32
            )

        sent = lax.ppermute(combined(1 - y).astype(BF16), "y", SWAP)
        return combined(y) + sent.astype(F32)

    routed = jnp.zeros((rows, features), F32)
    if zs <= 4:
        for shift, k, chunk in chunks:
            owner = (x + shift) % tp
            at = owner * zt + turn(owner, k)
            total = partial_sum(chunk, at)
            goals = [((i + shift) % tp) * zt + turn_of((i + shift) % tp, k) for i in range(tp)]
            for distance in range(zs - 1, 0, -1):
                sent = total.astype(BF16)
                first, second = {}, {}
                for i in range(tp):
                    for way in (1, -1):
                        start = goals[i] - way * distance
                        if 0 <= start < zs:
                            end = (start + way) * tp + i
                            (second if end in first else first)[end] = start * tp + i
                for links in (first, second):
                    if links:
                        moved = lax.ppermute(sent, ("z", "tp"), [(a, b) for b, a in links.items()])
                        total = total + moved.astype(F32)
            routed = jnp.where(z == at, total, routed)
    else:
        totals = jnp.zeros((zs, rows, features), BF16)
        for shift, k, chunk in chunks:
            owner = (x + shift) % tp
            at = owner * zt + turn(owner, k)
            totals = lax.dynamic_update_index_in_dim(totals, partial_sum(chunk, at).astype(BF16), at, 0)
        routed = lax.psum_scatter(totals, "z", scatter_dimension=0).astype(F32)

    sheet = sheet.reshape(tp, zt, 2 * rows, 2 * columns)
    dense = pick(sheet, x).astype(F32)
    for shift in range(1, tp):
        sent = pick(sheet, (x + shift) % tp)
        dense = dense + lax.ppermute(sent, "tp", [(i, (i + shift) % tp) for i in range(tp)]).astype(F32)
    dense = dense.reshape(zt, 2, rows, 2 * columns)
    theirs = lax.ppermute(dense[:, 1].astype(BF16), "y", SWAP).astype(F32)
    mine = dense[:, 0]
    both = jnp.stack([jnp.where(y == 0, mine, theirs), jnp.where(y == 0, theirs, mine)], 1)
    dense = jnp.moveaxis(both, 2, 0).reshape(rows, features)

    zero_gate = jnp.sum(jnp.where(expert_ids < experts, F32(0.0), gate_weights), axis=1)
    identity = zero_gate[:, None] * tokens.astype(F32)
    return (dense + routed + identity).astype(BF16)


def solution(mesh):
    groups, ranks, tp = mesh.devices.shape
    split = Mesh(mesh.devices.reshape(groups, ranks // 4, 2, 2, tp), ("grp", "z", "y", "c", "tp"))
    ep = ("z", "y", "c")
    return jax.shard_map(
        local,
        mesh=split,
        in_specs=(
            P(("grp",) + ep, "tp"),
            P(("grp",) + ep, None),
            P(("grp",) + ep, None),
            P(ep, ("grp", "tp"), None),
            P(ep, None, "tp"),
            P(("grp",) + ep, "tp"),
            P("tp", ep),
        ),
        out_specs=P(("grp",) + ep, "tp"),
        check_vma=False,
    )
```

```python
import jax
import jax.numpy as jnp
from jax import lax
from jax.experimental import pallas as pl
from jax.experimental.pallas import tpu as pltpu
from jax.sharding import Mesh, PartitionSpec as P

F32 = jnp.float32
BF16 = jnp.bfloat16
SWAP = ((0, 1), (1, 0))
FREE = pl.CostEstimate(flops=0, bytes_accessed=0, transcendentals=0)


def pick(array, index, axis=0):
    return lax.dynamic_index_in_dim(array, index, axis, keepdims=False)


def gate_rows(expert_ids, gate_weights, experts):
    ids, gates = expert_ids.T, gate_weights.T
    labels = jnp.arange(experts, dtype=jnp.int32)[:, None, None]
    return jnp.max(jnp.where(ids[None] == labels, gates[None], F32(-1.0)), axis=1)


def spread_gates(rows, zs, y, z):
    c = lax.axis_index("c")
    rows = rows.reshape(zs, 2, 2, rows.shape[-1])
    mine = pick(rows, y, 1)
    other = lax.ppermute(pick(rows, 1 - y, 1), "y", SWAP)
    both = jnp.stack([jnp.where(y == 0, mine, other), jnp.where(y == 0, other, mine)], 1)
    both = jnp.stack([pick(both, c, 2), pick(both, 1 - c, 2)], 2)
    got = [pick(both, z)]
    for shift in range(1, zs):
        got.append(lax.ppermute(pick(both, (z + shift) % zs), "z", [(i, (i + shift) % zs) for i in range(zs)]))
    got = jnp.stack(got)
    return jnp.stack([pick(got, (z - i) % zs) for i in range(zs)])


def placement(gates, capacity):
    tokens = gates.shape[-1]
    picked = gates >= 0
    order = jnp.arange(tokens)
    earlier = (order[:, None] < order[None, :]).astype(BF16)
    slots = jnp.dot(picked.astype(BF16), earlier, preferred_element_type=F32).astype(jnp.int32)
    slots = jnp.where(picked, slots, -1)
    places = jnp.arange(capacity, dtype=jnp.int32)
    table = jnp.where(slots[..., None] == places, gates[..., None], F32(0.0))
    table = jnp.moveaxis(table, -3, -2)
    table = table.reshape(table.shape[:-2] + (2 * capacity,))
    high = table.astype(BF16)
    low = (table - high.astype(F32)).astype(BF16)
    return high, low


def combine_kernel(at, gates, mine, sibling, out):
    capacity, tokens = mine.shape[1], gates.shape[2]
    steps = pl.num_programs(0)
    order = lax.broadcasted_iota(jnp.int32, (tokens, tokens), 0)
    earlier = (order < lax.broadcasted_iota(jnp.int32, (tokens, tokens), 1)).astype(BF16)
    places = lax.broadcasted_iota(jnp.int32, (capacity, tokens), 0)
    total = None
    for e, table in enumerate((mine, sibling)):
        gate = gates[0, pl.ds(at[3 * steps + e], 1), :]
        picked = gate >= 0
        marks = jnp.broadcast_to(jnp.where(picked, F32(1.0), F32(0.0)), (8, tokens)).astype(BF16)
        slot = jnp.dot(marks, earlier, preferred_element_type=F32)[0:1].astype(jnp.int32)
        place = jnp.where((slot == places) & picked, gate, F32(0.0))
        high = place.astype(BF16)
        low = (place - high.astype(F32)).astype(BF16)
        for part in (high, low):
            term = lax.dot_general(part, table[0], (((0,), (0,)), ((), ())), preferred_element_type=F32)
            total = term if total is None else total + term
    out[0] = total.astype(out.dtype)


def combine(at, steps, gates, table, sibling, dtype):
    _, capacity, features = table.shape
    tokens = gates.shape[2]
    return pl.pallas_call(
        combine_kernel,
        out_shape=jax.ShapeDtypeStruct((steps, tokens, features), dtype),
        grid_spec=pltpu.PrefetchScalarGridSpec(
            num_scalar_prefetch=1,
            grid=(steps,),
            in_specs=[
                pl.BlockSpec((1,) + gates.shape[1:], lambda i, at: (at[i], 0, 0)),
                pl.BlockSpec((1, capacity, features), lambda i, at: (at[steps + i], 0, 0)),
                pl.BlockSpec((1, capacity, features), lambda i, at: (at[2 * steps + i], 0, 0)),
            ],
            out_specs=pl.BlockSpec((1, tokens, features), lambda i, at: (i, 0, 0)),
        ),
        compiler_params=pltpu.CompilerParams(vmem_limit_bytes=32 << 20),
        cost_estimate=FREE,
    )(at, gates, table, sibling)


def tables_kernel(core, hidden, down, sent, kept):
    steps = pl.num_programs(0)
    value = jnp.dot(hidden[0, 0], down[...], preferred_element_type=F32).astype(sent.dtype)

    @pl.when(2 * pl.program_id(0) < steps)
    def _():
        sent[0] = value

    @pl.when(2 * pl.program_id(0) >= steps)
    def _():
        kept[0] = value


def expert_tables(core, hidden, down):
    blocks, _, capacity, units = hidden.shape
    features = down.shape[1]
    shape = jax.ShapeDtypeStruct((blocks, capacity, features), hidden.dtype)
    return pl.pallas_call(
        tables_kernel,
        out_shape=(shape, shape),
        grid_spec=pltpu.PrefetchScalarGridSpec(
            num_scalar_prefetch=1,
            grid=(2 * blocks,),
            in_specs=[
                pl.BlockSpec(
                    (1, 1, capacity, units),
                    lambda i, core: (lax.rem(i, blocks), jnp.where(i < blocks, 1 - core[0], core[0]), 0, 0),
                ),
                pl.BlockSpec((units, features), lambda i, core: (0, 0)),
            ],
            out_specs=[
                pl.BlockSpec((1, capacity, features), lambda i, core: (jnp.minimum(i, blocks - 1), 0, 0)),
                pl.BlockSpec((1, capacity, features), lambda i, core: (jnp.maximum(i - blocks, 0), 0, 0)),
            ],
        ),
        compiler_params=pltpu.CompilerParams(vmem_limit_bytes=32 << 20),
        cost_estimate=FREE,
    )(core, hidden, down)


def product_kernel(acts_a, acts_b, acts_c, acts_d, first, second, out):
    start = pl.program_id(0) == 0
    for w, weights in enumerate((first, second)):
        for i, acts in enumerate((acts_a, acts_b, acts_c, acts_d)):
            term = lax.dot_general(acts[...], weights[...], (((1,), (1,)), ((), ())), preferred_element_type=F32)
            out[w, i] = jnp.where(start, term, out[w, i] + term)


def products(acts, first, second):
    rows, depth = acts[0].shape
    columns = first.shape[0]
    step = depth // 4
    shape = (2, 4, rows, columns)
    return pl.pallas_call(
        product_kernel,
        out_shape=jax.ShapeDtypeStruct(shape, F32),
        grid=(depth // step,),
        in_specs=[pl.BlockSpec((rows, step), lambda i: (0, i))] * 4 + [pl.BlockSpec((columns, step), lambda i: (0, i))] * 2,
        out_specs=pl.BlockSpec(shape, lambda i: (0, 0, 0, 0)),
        compiler_params=pltpu.CompilerParams(vmem_limit_bytes=32 << 20),
        cost_estimate=FREE,
    )(*acts, first, second)


def four_by_two(tokens, expert_ids, gate_weights, expert_hidden, expert_down, dense_hidden, dense_down):
    z, y, c, x = (lax.axis_index(name) for name in ("z", "y", "c", "tp"))
    experts = 16
    rows = tokens.shape[0]
    hidden, down = expert_hidden[0], expert_down[0]
    capacity = hidden.shape[0] // 8
    features = down.shape[1]
    columns = dense_down.shape[1]
    right = [(0, 1), (1, 2), (2, 3)]
    left = [(1, 0), (2, 1), (3, 2)]
    tie = lax.optimization_barrier

    core = jnp.reshape(c, (1,))

    def tables(chunk):
        sent, kept = expert_tables(core, chunk.reshape(-1, 2, capacity, chunk.shape[-1]), down)
        return kept, lax.ppermute(sent, "c", SWAP)

    def sums(tables, gates, goals, away, dtype):
        side = 1 - y if away else y
        at = [goal * 2 + side for goal, _ in goals]
        at += [place * 2 + side for _, place in goals] * 2
        at = jnp.stack(at + [c, 1 - c]).astype(jnp.int32)
        return combine(at, len(goals), gates, *tables, dtype)

    halves = hidden.reshape(2, 4 * capacity, hidden.shape[1])
    hidden_0 = lax.ppermute(pick(halves, x), "tp", SWAP)
    weights = dense_down.T
    weights_r1 = lax.ppermute(weights, "z", right)
    weights_l1 = lax.ppermute(weights, "z", left)
    acts_y = lax.ppermute(dense_hidden, "y", SWAP)
    gates = gate_rows(expert_ids, gate_weights, experts).reshape(8, 2, rows)
    gates = lax.all_to_all(gates, ("z", "y"), 0, 0, tiled=True)
    own = tables(hidden)
    own_goals = ((3 * x, x), (1 + x, 1 - x))
    given_own = sums(own, gates, own_goals, 1, BF16)
    given_own, acts_y, acts_c = tie((given_own, acts_y, dense_hidden))
    acts_c = lax.ppermute(acts_c, "c", SWAP)
    got_own = lax.ppermute(given_own, "y", SWAP)
    acts_cy = lax.ppermute(acts_y, "c", SWAP)
    acts = (dense_hidden, acts_y, acts_c, acts_cy)

    hidden_1, hidden_0, weights_r1, weights_l1 = tie((pick(halves, 1 - x), hidden_0, weights_r1, weights_l1))
    hidden_1 = lax.ppermute(hidden_1, "tp", SWAP)
    weights_r2 = lax.ppermute(weights_r1, "z", right)
    weights_l2 = lax.ppermute(weights_l1, "z", left)
    outer = tables(hidden_0)
    given_outer = sums(outer, gates, ((3 * (1 - x), 0),), 1, BF16)
    given_outer, got_own = tie((given_outer, got_own))
    got_outer = lax.ppermute(given_outer, "y", SWAP)
    sum_own = sums(own, gates, own_goals, 0, F32) + got_own.astype(F32)
    sheets = [products(acts, weights, weights), products(acts, weights_r1, weights_l1)]

    weights_r2, weights_l2, hidden_1, sheets = tie((weights_r2, weights_l2, hidden_1, sheets))
    weights_r3 = lax.ppermute(weights_r2, "z", right)
    weights_l3 = lax.ppermute(weights_l2, "z", left)
    inner = tables(hidden_1)
    given_inner = sums(inner, gates, ((2 - x, 0),), 1, BF16)
    given_inner, got_outer = tie((given_inner, got_outer))
    got_inner = lax.ppermute(given_inner, "y", SWAP)
    sum_outer = (sums(outer, gates, ((3 * (1 - x), 0),), 0, F32) + got_outer.astype(F32))[0]
    goal_0 = jnp.where(x == 0, sum_own[0], sum_outer)
    goal_3 = jnp.where(x == 0, sum_outer, sum_own[0])
    up = lax.ppermute(goal_3.astype(BF16), "z", [(0, 1)])
    low = lax.ppermute(goal_0.astype(BF16), "z", [(3, 2)])
    sheets = sheets + [products(acts, weights_r2, weights_l2)]
    sum_inner = (sums(inner, gates, ((2 - x, 0),), 0, F32) + got_inner.astype(F32))[0]
    goal_1 = jnp.where(x == 0, sum_own[1], sum_inner)
    goal_2 = jnp.where(x == 0, sum_inner, sum_own[1])

    up = jnp.where(z == 0, goal_2, goal_3 + up.astype(F32)).astype(BF16)
    low = jnp.where(z == 3, goal_1, goal_0 + low.astype(F32)).astype(BF16)
    up, low, weights_r3, weights_l3, sheets = tie((up, low, weights_r3, weights_l3, sheets))
    up = lax.ppermute(up, "z", [(0, 1), (1, 2)])
    low = lax.ppermute(low, "z", [(3, 2), (2, 1)])
    sheets = sheets + [products(acts, weights_r3, weights_l3)]
    sheet = [sheets[i][0] for i in (3, 2, 1, 0)] + [sheets[i][1] for i in (1, 2, 3)]
    sheet = jnp.stack(sheet)
    theirs = lax.dynamic_slice_in_dim(sheet, 3 - z + 2 * (1 - x), 2).astype(BF16)
    dense = lax.dynamic_slice_in_dim(sheet, 3 - z + 2 * x, 2)
    dense = dense + lax.ppermute(theirs, "tp", SWAP).astype(F32)

    up = jnp.where(z == 0, goal_1, jnp.where(z == 1, goal_2, goal_3) + up.astype(F32)).astype(BF16)
    low = jnp.where(z == 3, goal_2, jnp.where(z == 2, goal_1, goal_0) + low.astype(F32)).astype(BF16)
    up = lax.ppermute(up, "z", right)
    low = lax.ppermute(low, "z", left)
    routed = jnp.where(z == 0, goal_0, jnp.where(z == 1, goal_1, jnp.where(z == 2, goal_2, goal_3)))
    routed = routed + (up.astype(F32) + low.astype(F32))

    dense = dense.reshape(2, 2, 2, rows, columns)
    near = dense[:, 0, 0]
    by_c = lax.ppermute(dense[:, 1, 0].astype(BF16), "c", SWAP).astype(F32)
    by_y = lax.ppermute(dense[:, 0, 1].astype(BF16), "y", SWAP).astype(F32)
    by_both = lax.ppermute(dense[:, 1, 1].astype(BF16), ("y", "c"), [(0, 3), (1, 2), (2, 1), (3, 0)]).astype(F32)

    def ordered(first, second, swap):
        return jnp.where(swap, second, first), jnp.where(swap, first, second)

    same = jnp.concatenate(ordered(near, by_c, c == 1), 2)
    across = jnp.concatenate(ordered(by_y, by_both, c == 1), 2)
    pair = ordered(same, across, y == 1)
    dense = jnp.concatenate([pair[0][0], pair[1][0], pair[0][1], pair[1][1]], 1)

    zero_gate = jnp.sum(jnp.where(expert_ids < experts, F32(0.0), gate_weights), axis=1)
    identity = zero_gate[:, None] * tokens.astype(F32)
    return (dense + routed + identity).astype(BF16)


def any_mesh(tokens, expert_ids, gate_weights, expert_hidden, expert_down, dense_hidden, dense_down):
    zs, tp = lax.axis_size("z"), lax.axis_size("tp")
    z, y, c, x = (lax.axis_index(name) for name in ("z", "y", "c", "tp"))
    experts = zs * 4
    zt = zs // tp
    rows = tokens.shape[0]
    hidden, down = expert_hidden[0], expert_down[0]
    capacity = hidden.shape[0] // (zt * 4)
    features = down.shape[1]

    hidden = hidden.reshape(zt, 4 * capacity, hidden.shape[1])

    def turn(owner, k):
        return jnp.where(2 * owner < tp, k, zt - 1 - k)

    chunks = []
    for k in range(zt):
        chunks.append((0, k, pick(hidden, turn(x, k))))
    for shift in range(1, tp):
        for k in range(zt):
            sent = chunks[k][2]
            moved = lax.ppermute(sent, "tp", [((i + shift) % tp, i) for i in range(tp)])
            chunks.append((shift, k, moved))

    acts = jnp.stack([dense_hidden, lax.ppermute(dense_hidden, "y", SWAP)])
    acts = acts.reshape(2 * rows, -1)
    columns = dense_down.shape[1]

    def product(weights):
        sibling = lax.ppermute(weights, "c", SWAP)
        first = jnp.where(c == 0, weights, sibling)
        second = jnp.where(c == 0, sibling, weights)
        both = jnp.concatenate([first, second], 1)
        return jnp.dot(acts, both, preferred_element_type=F32).astype(BF16)

    sheet = jnp.zeros((zs, 2 * rows, 2 * columns), BF16)
    every = lax.all_gather(dense_down, "z")
    for i in range(zs):
        sheet = lax.dynamic_update_index_in_dim(sheet, product(every[i]), i, 0)

    gates = spread_gates(gate_rows(expert_ids, gate_weights, experts), zs, y, z)
    high, low = placement(gates, capacity)

    def partial_sum(chunk, at):
        out = jnp.dot(chunk, down, preferred_element_type=F32).astype(BF16)
        out = out.reshape(2, 2, capacity, features)
        sibling = lax.ppermute(pick(out, 1 - c, 1), "c", SWAP)
        table = jnp.concatenate([pick(out, c, 1), sibling], 1)
        p_high, p_low = pick(high, at), pick(low, at)

        def combined(which):
            t = pick(table, which)
            return jnp.dot(pick(p_high, which), t, preferred_element_type=F32) + jnp.dot(
                pick(p_low, which), t, preferred_element_type=F32
            )

        sent = lax.ppermute(combined(1 - y).astype(BF16), "y", SWAP)
        return combined(y) + sent.astype(F32)

    totals = jnp.zeros((zs, rows, features), BF16)
    for shift, k, chunk in chunks:
        owner = (x + shift) % tp
        at = owner * zt + turn(owner, k)
        totals = lax.dynamic_update_index_in_dim(totals, partial_sum(chunk, at).astype(BF16), at, 0)
    routed = lax.psum_scatter(totals, "z", scatter_dimension=0).astype(F32)

    sheet = sheet.reshape(tp, zt, 2 * rows, 2 * columns)
    dense = pick(sheet, x).astype(F32)
    for shift in range(1, tp):
        sent = pick(sheet, (x + shift) % tp)
        dense = dense + lax.ppermute(sent, "tp", [(i, (i + shift) % tp) for i in range(tp)]).astype(F32)
    dense = dense.reshape(zt, 2, rows, 2 * columns)
    theirs = lax.ppermute(dense[:, 1].astype(BF16), "y", SWAP).astype(F32)
    mine = dense[:, 0]
    both = jnp.stack([jnp.where(y == 0, mine, theirs), jnp.where(y == 0, theirs, mine)], 1)
    dense = jnp.moveaxis(both, 2, 0).reshape(rows, features)

    zero_gate = jnp.sum(jnp.where(expert_ids < experts, F32(0.0), gate_weights), axis=1)
    identity = zero_gate[:, None] * tokens.astype(F32)
    return (dense + routed + identity).astype(BF16)


def solution(mesh):
    groups, ranks, tp = mesh.devices.shape
    split = Mesh(mesh.devices.reshape(groups, ranks // 4, 2, 2, tp), ("grp", "z", "y", "c", "tp"))
    ep = ("z", "y", "c")
    return jax.shard_map(
        four_by_two if ranks == 16 and tp == 2 else any_mesh,
        mesh=split,
        in_specs=(
            P(("grp",) + ep, "tp"),
            P(("grp",) + ep, None),
            P(("grp",) + ep, None),
            P(ep, ("grp", "tp"), None),
            P(ep, None, "tp"),
            P(("grp",) + ep, "tp"),
            P("tp", ep),
        ),
        out_specs=P(("grp",) + ep, "tp"),
        check_vma=False,
    )
```

```python
import jax
import jax.numpy as jnp
from jax import lax
from jax.experimental import pallas as pl
from jax.experimental.pallas import tpu as pltpu
from jax.sharding import Mesh, PartitionSpec as P

F32 = jnp.float32
BF16 = jnp.bfloat16
SWAP = ((0, 1), (1, 0))
VMEM = 32 << 20
FREE = pl.CostEstimate(flops=0, bytes_accessed=0, transcendentals=0)


def pick(array, index, axis=0):
    return lax.dynamic_index_in_dim(array, index, axis, keepdims=False)


def gate_rows(expert_ids, gate_weights, experts):
    ids, gates = expert_ids.T, gate_weights.T
    labels = jnp.arange(experts, dtype=jnp.int32)[:, None, None]
    return jnp.max(jnp.where(ids[None] == labels, gates[None], F32(-1.0)), axis=1)


def spread_gates(rows, zs, y, z):
    c = lax.axis_index("c")
    rows = rows.reshape(zs, 2, 2, rows.shape[-1])
    mine = pick(rows, y, 1)
    other = lax.ppermute(pick(rows, 1 - y, 1), "y", SWAP)
    both = jnp.stack([jnp.where(y == 0, mine, other), jnp.where(y == 0, other, mine)], 1)
    both = jnp.stack([pick(both, c, 2), pick(both, 1 - c, 2)], 2)
    got = [pick(both, z)]
    for shift in range(1, zs):
        got.append(lax.ppermute(pick(both, (z + shift) % zs), "z", [(i, (i + shift) % zs) for i in range(zs)]))
    got = jnp.stack(got)
    return jnp.stack([pick(got, (z - i) % zs) for i in range(zs)])


def placement(gates, capacity):
    tokens = gates.shape[-1]
    picked = gates >= 0
    order = jnp.arange(tokens)
    earlier = (order[:, None] < order[None, :]).astype(BF16)
    slots = jnp.dot(picked.astype(BF16), earlier, preferred_element_type=F32).astype(jnp.int32)
    slots = jnp.where(picked, slots, -1)
    places = jnp.arange(capacity, dtype=jnp.int32)
    table = jnp.where(slots[..., None] == places, gates[..., None], F32(0.0))
    table = jnp.moveaxis(table, -3, -2)
    table = table.reshape(table.shape[:-2] + (2 * capacity,))
    high = table.astype(BF16)
    low = (table - high.astype(F32)).astype(BF16)
    return high, low


def combine_kernel(here, gates, columns, mine, sibling, out):
    capacity, tokens = mine.shape[1], gates.shape[2]
    order = lax.broadcasted_iota(jnp.int32, (tokens, tokens), 0)
    earlier = (order < lax.broadcasted_iota(jnp.int32, (tokens, tokens), 1)).astype(BF16)
    places = lax.broadcasted_iota(jnp.int32, (capacity, tokens), 0)
    c = here[2]
    total = None
    for e, table in ((c, mine), (1 - c, sibling)):
        picked = gates[0, pl.ds(e, 1), :] >= 0
        marks = jnp.broadcast_to(jnp.where(picked, F32(1.0), F32(0.0)), (8, tokens)).astype(BF16)
        slot = jnp.dot(marks, earlier, preferred_element_type=F32)[0:1].astype(jnp.int32)
        place = jnp.where((slot == places) & picked, F32(1.0), F32(0.0)).astype(BF16)
        term = lax.dot_general(place, table[0], (((0,), (0,)), ((), ())), preferred_element_type=F32)
        term = jnp.where(e == 0, columns[0, :, 0:1], columns[0, :, 1:2]) * term
        total = term if total is None else total + term
    out[...] = total.astype(out.dtype)


def combine(here, goal, place, away, gates, columns, table, sibling, dtype):
    _, capacity, features = table.shape
    tokens = gates.shape[2]

    def gate_block(i, here):
        return goal(here[0]) * 2 + (1 - here[1] if away else here[1]), 0, 0

    def table_block(i, here):
        return place(here[0]) * 2 + (1 - here[1] if away else here[1]), 0, 0

    return pl.pallas_call(
        combine_kernel,
        out_shape=jax.ShapeDtypeStruct((tokens, features), dtype),
        grid_spec=pltpu.PrefetchScalarGridSpec(
            num_scalar_prefetch=1,
            grid=(1,),
            in_specs=[
                pl.BlockSpec((1,) + gates.shape[1:], gate_block),
                pl.BlockSpec((1,) + columns.shape[1:], gate_block),
                pl.BlockSpec((1, capacity, features), table_block),
                pl.BlockSpec((1, capacity, features), table_block),
            ],
            out_specs=pl.BlockSpec((tokens, features), lambda i, here: (0, 0)),
        ),
        compiler_params=pltpu.CompilerParams(vmem_limit_bytes=VMEM),
        cost_estimate=FREE,
    )(here, gates, columns, table, sibling)


def tables_kernel(here, hidden, down, sent, kept):
    steps = pl.num_programs(0)
    value = jnp.dot(hidden[0, 0], down[...], preferred_element_type=F32).astype(sent.dtype)

    @pl.when(2 * pl.program_id(0) < steps)
    def _():
        sent[0] = value

    @pl.when(2 * pl.program_id(0) >= steps)
    def _():
        kept[0] = value


def expert_tables(here, hidden, down):
    blocks, _, capacity, units = hidden.shape
    features = down.shape[1]
    shape = jax.ShapeDtypeStruct((blocks, capacity, features), hidden.dtype)
    return pl.pallas_call(
        tables_kernel,
        out_shape=(shape, shape),
        grid_spec=pltpu.PrefetchScalarGridSpec(
            num_scalar_prefetch=1,
            grid=(2 * blocks,),
            in_specs=[
                pl.BlockSpec(
                    (1, 1, capacity, units),
                    lambda i, here: (lax.rem(i, blocks), jnp.where(i < blocks, 1 - here[2], here[2]), 0, 0),
                ),
                pl.BlockSpec((units, features), lambda i, here: (0, 0)),
            ],
            out_specs=[
                pl.BlockSpec((1, capacity, features), lambda i, here: (jnp.minimum(i, blocks - 1), 0, 0)),
                pl.BlockSpec((1, capacity, features), lambda i, here: (jnp.maximum(i - blocks, 0), 0, 0)),
            ],
        ),
        compiler_params=pltpu.CompilerParams(vmem_limit_bytes=VMEM),
        cost_estimate=FREE,
    )(here, hidden, down)


def products_kernel(acts_a, acts_b, acts_c, acts_d, *weights_and_outs):
    start = pl.program_id(0) == 0
    count = len(weights_and_outs) // 2
    for weights, out in zip(weights_and_outs[:count], weights_and_outs[count:]):
        for i, acts in enumerate((acts_a, acts_b, acts_c, acts_d)):
            term = lax.dot_general(acts[...], weights[...], (((1,), (1,)), ((), ())), preferred_element_type=F32)
            out[i] = jnp.where(start, term, out[i] + term)


def products(acts, *weights):
    rows, depth = acts[0].shape
    columns = weights[0].shape[0]
    step = depth // 4
    shape = (4, rows, columns)
    count = len(weights)
    return pl.pallas_call(
        products_kernel,
        out_shape=[jax.ShapeDtypeStruct(shape, F32)] * count,
        grid=(depth // step,),
        in_specs=[pl.BlockSpec((rows, step), lambda i: (0, i))] * 4
        + [pl.BlockSpec((columns, step), lambda i: (0, i))] * count,
        out_specs=[pl.BlockSpec(shape, lambda i: (0, 0, 0))] * count,
        compiler_params=pltpu.CompilerParams(vmem_limit_bytes=VMEM),
        cost_estimate=FREE,
    )(*acts, *weights)


def four_by_two(tokens, expert_ids, gate_weights, expert_hidden, expert_down, dense_hidden, dense_down):
    z, y, c, x = (lax.axis_index(name) for name in ("z", "y", "c", "tp"))
    experts = 16
    rows = tokens.shape[0]
    hidden, down = expert_hidden[0], expert_down[0]
    capacity = hidden.shape[0] // 8
    features = down.shape[1]
    columns = dense_down.shape[1]
    right = [(0, 1), (1, 2), (2, 3)]
    left = [(1, 0), (2, 1), (3, 2)]
    tie = lax.optimization_barrier

    here = jnp.stack([x, y, c]).astype(jnp.int32)

    def tables(chunk):
        return expert_tables(here, chunk.reshape(-1, 2, capacity, chunk.shape[-1]), down)

    def over_c(value):
        return lax.ppermute(value, "c", SWAP)

    def sums(tables, gates, goal, away, dtype):
        return combine(here, *goal, away, *gates, *tables, dtype)

    def hop(value, *ways):
        pairs = [(i * 2 + at, j * 2 + at) for at in range(2) for i, j in ways[at]]
        return lax.ppermute(value.astype(BF16), ("z", "tp"), pairs)

    def over_y(value):
        return lax.ppermute(value, "y", SWAP)

    own_goals = (lambda x: 3 * x, lambda x: x), (lambda x: 1 + x, lambda x: 1 - x)
    outer_goal = lambda x: 3 * (1 - x), lambda x: 0
    inner_goal = lambda x: 2 - x, lambda x: 0
    far = jnp.where(x == 0, 3, 0)
    distance = jnp.abs(z - far)

    halves = hidden.reshape(2, 4 * capacity, hidden.shape[1])
    weights = dense_down.T
    gates = gate_rows(expert_ids, gate_weights, experts).reshape(8, 2, rows)
    weights, hidden_0, gates = tie((weights, pick(halves, x), gates))
    weights_r1 = lax.ppermute(weights, "z", right)
    weights_l1 = lax.ppermute(weights, "z", left)
    hidden_0 = lax.ppermute(hidden_0, "tp", SWAP)
    acts_y = over_y(dense_hidden)
    acts_c = over_c(dense_hidden)
    gates = lax.all_to_all(gates, ("z", "y"), 0, 0, tiled=True)
    own_sent, own = tables(hidden)
    hidden_1 = pick(halves, 1 - x)
    gates = gates, jnp.swapaxes(gates, 1, 2)
    hidden_0, acts_y, weights_r1, weights_l1, gates, own, own_sent, hidden_1, acts_c = tie(
        (hidden_0, acts_y, weights_r1, weights_l1, gates, own, own_sent, hidden_1, acts_c)
    )
    own = own, over_c(own_sent)

    weights_r2 = lax.ppermute(weights_r1, "z", right[1:])
    weights_l2 = lax.ppermute(weights_l1, "z", left[:2])
    hidden_1 = lax.ppermute(hidden_1, "tp", SWAP)
    got_own_0 = over_y(sums(own, gates, own_goals[0], 1, BF16))
    sum_own_0 = sums(own, gates, own_goals[0], 0, F32)
    outer_sent, outer = tables(hidden_0)
    outer = outer, over_c(outer_sent)
    got_own_0, given_outer, sum_own_0 = tie((got_own_0, sums(outer, gates, outer_goal, 1, BF16), sum_own_0))

    got_outer = over_y(given_outer)
    own_0 = sum_own_0 + got_own_0.astype(F32)
    own_a = hop(own_0, [(3, 2)], [(0, 1)])
    sum_outer = sums(outer, gates, outer_goal, 0, F32)
    given_own_1 = sums(own, gates, own_goals[1], 1, BF16)
    got_outer, own_a, weights_r2, weights_l2, hidden_1, given_own_1, sum_outer, own_0, acts_y = tie(
        (got_outer, own_a, weights_r2, weights_l2, hidden_1, given_own_1, sum_outer, own_0, acts_y)
    )

    weights_r3 = lax.ppermute(weights_r2, "z", right[2:])
    weights_l3 = lax.ppermute(weights_l2, "z", left[:1])
    got_own_1 = over_y(given_own_1)
    outer_0 = sum_outer + got_outer.astype(F32)
    other_a = hop(outer_0, [(0, 1)], [(3, 2)])
    inner_sent, inner = tables(hidden_1)
    inner = inner, over_c(inner_sent)
    sum_own_1 = sums(own, gates, own_goals[1], 0, F32)
    got_own_1, given_inner, acts_y, sum_own_1 = tie((got_own_1, sums(inner, gates, inner_goal, 1, BF16), acts_y, sum_own_1))

    got_inner = over_y(given_inner)
    acts = (dense_hidden, acts_y, acts_c, over_c(acts_y))
    sum_inner = sums(inner, gates, inner_goal, 0, F32)
    second = jnp.where(z == 0, weights_l1, weights_r1)
    third = jnp.where(z == 0, weights_l2, jnp.where(z == 3, weights_r2, weights_l1))
    fourth = jnp.where(z == 1, weights_l2, weights_r2)
    sheet = tuple(products(acts, weights, second, third))
    weights_r3, weights_l3, other_a, got_own_1, got_inner, sum_inner, sheet, fourth, own_0, outer_0 = tie(
        (weights_r3, weights_l3, other_a, got_own_1, got_inner, sum_inner, sheet, fourth, own_0, outer_0)
    )

    own_1 = sum_own_1 + got_own_1.astype(F32)
    inner_0 = sum_inner + got_inner.astype(F32)
    (last,) = products(acts, jnp.where(z == 0, weights_l3, jnp.where(z == 3, weights_r3, fourth)))
    s_0, s_1, s_2 = sheet
    of_z = [
        jnp.where(z == 0, s_0, jnp.where(z == 1, s_1, last)),
        jnp.where(z == 1, s_0, jnp.where(z == 3, s_2, s_1)),
        jnp.where(z == 2, s_0, jnp.where(z == 3, s_1, s_2)),
        jnp.where(z == 3, s_0, jnp.where(z == 2, s_2, last)),
    ]
    theirs = jnp.stack([jnp.where(x == 0, of_z[2], of_z[0]), jnp.where(x == 0, of_z[3], of_z[1])]).astype(BF16)
    dense = jnp.stack([jnp.where(x == 0, of_z[0], of_z[2]), jnp.where(x == 0, of_z[1], of_z[3])])
    theirs = lax.ppermute(theirs, "tp", SWAP)
    own_b = hop(jnp.where(z == far, own_1, own_0 + own_a.astype(F32)), [(3, 2), (2, 1)], [(0, 1), (1, 2)])
    other_b = jnp.where(z == 3 - far, inner_0, outer_0 + other_a.astype(F32))
    other_b = hop(other_b, [(0, 1), (1, 2)], [(3, 2), (2, 1)])
    own_b, other_b, theirs, dense, own_1, inner_0 = tie((own_b, other_b, theirs, dense, own_1, inner_0))
    dense = dense + theirs.astype(F32)

    own_c = jnp.where(z == far, inner_0, own_b.astype(F32) + jnp.where(distance == 1, own_1, own_0))
    own_c = hop(own_c, left, right)
    other_c = jnp.where(z == 3 - far, own_1, other_b.astype(F32) + jnp.where(distance == 2, inner_0, outer_0))
    other_c = hop(other_c, right, left)
    routed = jnp.where(distance == 3, own_0, jnp.where(distance == 2, own_1, jnp.where(distance == 1, inner_0, outer_0)))
    routed = routed + own_c.astype(F32) + other_c.astype(F32)

    dense = dense.reshape(2, 2, 2, rows, columns)
    near = dense[:, 0, 0]
    by_c = lax.ppermute(dense[:, 1, 0].astype(BF16), "c", SWAP).astype(F32)
    by_y = lax.ppermute(dense[:, 0, 1].astype(BF16), "y", SWAP).astype(F32)
    by_both = lax.ppermute(dense[:, 1, 1].astype(BF16), ("y", "c"), [(0, 3), (1, 2), (2, 1), (3, 0)]).astype(F32)

    def ordered(first, second, swap):
        return jnp.where(swap, second, first), jnp.where(swap, first, second)

    same = jnp.concatenate(ordered(near, by_c, c == 1), 2)
    across = jnp.concatenate(ordered(by_y, by_both, c == 1), 2)
    pair = ordered(same, across, y == 1)
    dense = jnp.concatenate([pair[0][0], pair[1][0], pair[0][1], pair[1][1]], 1)

    zero_gate = jnp.sum(jnp.where(expert_ids < experts, F32(0.0), gate_weights), axis=1)
    identity = zero_gate[:, None] * tokens.astype(F32)
    return (dense + routed + identity).astype(BF16)


def any_mesh(tokens, expert_ids, gate_weights, expert_hidden, expert_down, dense_hidden, dense_down):
    zs, tp = lax.axis_size("z"), lax.axis_size("tp")
    z, y, c, x = (lax.axis_index(name) for name in ("z", "y", "c", "tp"))
    experts = zs * 4
    zt = zs // tp
    rows = tokens.shape[0]
    hidden, down = expert_hidden[0], expert_down[0]
    capacity = hidden.shape[0] // (zt * 4)
    features = down.shape[1]

    hidden = hidden.reshape(zt, 4 * capacity, hidden.shape[1])

    def turn(owner, k):
        return jnp.where(2 * owner < tp, k, zt - 1 - k)

    chunks = []
    for k in range(zt):
        chunks.append((0, k, pick(hidden, turn(x, k))))
    for shift in range(1, tp):
        for k in range(zt):
            sent = chunks[k][2]
            moved = lax.ppermute(sent, "tp", [((i + shift) % tp, i) for i in range(tp)])
            chunks.append((shift, k, moved))

    acts = jnp.stack([dense_hidden, lax.ppermute(dense_hidden, "y", SWAP)])
    acts = acts.reshape(2 * rows, -1)
    columns = dense_down.shape[1]

    def product(weights):
        sibling = lax.ppermute(weights, "c", SWAP)
        first = jnp.where(c == 0, weights, sibling)
        second = jnp.where(c == 0, sibling, weights)
        both = jnp.concatenate([first, second], 1)
        return jnp.dot(acts, both, preferred_element_type=F32).astype(BF16)

    sheet = jnp.zeros((zs, 2 * rows, 2 * columns), BF16)
    every = lax.all_gather(dense_down, "z")
    for i in range(zs):
        sheet = lax.dynamic_update_index_in_dim(sheet, product(every[i]), i, 0)

    gates = spread_gates(gate_rows(expert_ids, gate_weights, experts), zs, y, z)
    high, low = placement(gates, capacity)

    def partial_sum(chunk, at):
        out = jnp.dot(chunk, down, preferred_element_type=F32).astype(BF16)
        out = out.reshape(2, 2, capacity, features)
        sibling = lax.ppermute(pick(out, 1 - c, 1), "c", SWAP)
        table = jnp.concatenate([pick(out, c, 1), sibling], 1)
        p_high, p_low = pick(high, at), pick(low, at)

        def combined(which):
            t = pick(table, which)
            return jnp.dot(pick(p_high, which), t, preferred_element_type=F32) + jnp.dot(
                pick(p_low, which), t, preferred_element_type=F32
            )

        sent = lax.ppermute(combined(1 - y).astype(BF16), "y", SWAP)
        return combined(y) + sent.astype(F32)

    totals = jnp.zeros((zs, rows, features), BF16)
    for shift, k, chunk in chunks:
        owner = (x + shift) % tp
        at = owner * zt + turn(owner, k)
        totals = lax.dynamic_update_index_in_dim(totals, partial_sum(chunk, at).astype(BF16), at, 0)
    routed = lax.psum_scatter(totals, "z", scatter_dimension=0).astype(F32)

    sheet = sheet.reshape(tp, zt, 2 * rows, 2 * columns)
    dense = pick(sheet, x).astype(F32)
    for shift in range(1, tp):
        sent = pick(sheet, (x + shift) % tp)
        dense = dense + lax.ppermute(sent, "tp", [(i, (i + shift) % tp) for i in range(tp)]).astype(F32)
    dense = dense.reshape(zt, 2, rows, 2 * columns)
    theirs = lax.ppermute(dense[:, 1].astype(BF16), "y", SWAP).astype(F32)
    mine = dense[:, 0]
    both = jnp.stack([jnp.where(y == 0, mine, theirs), jnp.where(y == 0, theirs, mine)], 1)
    dense = jnp.moveaxis(both, 2, 0).reshape(rows, features)

    zero_gate = jnp.sum(jnp.where(expert_ids < experts, F32(0.0), gate_weights), axis=1)
    identity = zero_gate[:, None] * tokens.astype(F32)
    return (dense + routed + identity).astype(BF16)


def solution(mesh):
    groups, ranks, tp = mesh.devices.shape
    split = Mesh(mesh.devices.reshape(groups, ranks // 4, 2, 2, tp), ("grp", "z", "y", "c", "tp"))
    ep = ("z", "y", "c")
    return jax.shard_map(
        four_by_two if ranks == 16 and tp == 2 else any_mesh,
        mesh=split,
        in_specs=(
            P(("grp",) + ep, "tp"),
            P(("grp",) + ep, None),
            P(("grp",) + ep, None),
            P(ep, ("grp", "tp"), None),
            P(ep, None, "tp"),
            P(("grp",) + ep, "tp"),
            P("tp", ep),
        ),
        out_specs=P(("grp",) + ep, "tp"),
        check_vma=False,
    )
```

```python
import jax
import jax.numpy as jnp
from jax import lax
from jax.experimental import pallas as pl
from jax.experimental.pallas import tpu as pltpu
from jax.sharding import Mesh, PartitionSpec as P

F32 = jnp.float32
BF16 = jnp.bfloat16
SWAP = ((0, 1), (1, 0))
VMEM = 32 << 20
FREE = pl.CostEstimate(flops=0, bytes_accessed=0, transcendentals=0)


def pick(array, index, axis=0):
    return lax.dynamic_index_in_dim(array, index, axis, keepdims=False)


def gate_rows(expert_ids, gate_weights, experts):
    ids, gates = expert_ids.T, gate_weights.T
    labels = jnp.arange(experts, dtype=jnp.int32)[:, None, None]
    return jnp.max(jnp.where(ids[None] == labels, gates[None], F32(-1.0)), axis=1)


def spread_gates(rows, zs, y, z):
    c = lax.axis_index("c")
    rows = rows.reshape(zs, 2, 2, rows.shape[-1])
    mine = pick(rows, y, 1)
    other = lax.ppermute(pick(rows, 1 - y, 1), "y", SWAP)
    both = jnp.stack([jnp.where(y == 0, mine, other), jnp.where(y == 0, other, mine)], 1)
    both = jnp.stack([pick(both, c, 2), pick(both, 1 - c, 2)], 2)
    got = [pick(both, z)]
    for shift in range(1, zs):
        got.append(lax.ppermute(pick(both, (z + shift) % zs), "z", [(i, (i + shift) % zs) for i in range(zs)]))
    got = jnp.stack(got)
    return jnp.stack([pick(got, (z - i) % zs) for i in range(zs)])


def placement(gates, capacity):
    tokens = gates.shape[-1]
    picked = gates >= 0
    order = jnp.arange(tokens)
    earlier = (order[:, None] < order[None, :]).astype(BF16)
    slots = jnp.dot(picked.astype(BF16), earlier, preferred_element_type=F32).astype(jnp.int32)
    slots = jnp.where(picked, slots, -1)
    places = jnp.arange(capacity, dtype=jnp.int32)
    table = jnp.where(slots[..., None] == places, gates[..., None], F32(0.0))
    table = jnp.moveaxis(table, -3, -2)
    table = table.reshape(table.shape[:-2] + (2 * capacity,))
    high = table.astype(BF16)
    low = (table - high.astype(F32)).astype(BF16)
    return high, low


def combine_kernel(here, gates, columns, mine, sibling, out):
    capacity, tokens = mine.shape[1], gates.shape[2]
    order = lax.broadcasted_iota(jnp.int32, (tokens, tokens), 0)
    earlier = (order < lax.broadcasted_iota(jnp.int32, (tokens, tokens), 1)).astype(BF16)
    places = lax.broadcasted_iota(jnp.int32, (capacity, tokens), 0)
    c = here[2]
    total = None
    for e, table in ((c, mine), (1 - c, sibling)):
        picked = gates[0, pl.ds(e, 1), :] >= 0
        marks = jnp.broadcast_to(jnp.where(picked, F32(1.0), F32(0.0)), (8, tokens)).astype(BF16)
        slot = jnp.dot(marks, earlier, preferred_element_type=F32)[0:1].astype(jnp.int32)
        place = jnp.where((slot == places) & picked, F32(1.0), F32(0.0)).astype(BF16)
        term = lax.dot_general(place, table[0], (((0,), (0,)), ((), ())), preferred_element_type=F32)
        term = jnp.where(e == 0, columns[0, :, 0:1], columns[0, :, 1:2]) * term
        total = term if total is None else total + term
    out[...] = total.astype(out.dtype)


def combine(here, goal, place, away, gates, columns, table, sibling, dtype):
    _, capacity, features = table.shape
    tokens = gates.shape[2]

    def gate_block(i, here):
        return goal(here[0]) * 2 + (1 - here[1] if away else here[1]), 0, 0

    def table_block(i, here):
        return place(here[0]) * 2 + (1 - here[1] if away else here[1]), 0, 0

    return pl.pallas_call(
        combine_kernel,
        out_shape=jax.ShapeDtypeStruct((tokens, features), dtype),
        grid_spec=pltpu.PrefetchScalarGridSpec(
            num_scalar_prefetch=1,
            grid=(1,),
            in_specs=[
                pl.BlockSpec((1,) + gates.shape[1:], gate_block),
                pl.BlockSpec((1,) + columns.shape[1:], gate_block),
                pl.BlockSpec((1, capacity, features), table_block),
                pl.BlockSpec((1, capacity, features), table_block),
            ],
            out_specs=pl.BlockSpec((tokens, features), lambda i, here: (0, 0)),
        ),
        compiler_params=pltpu.CompilerParams(vmem_limit_bytes=VMEM),
        cost_estimate=FREE,
    )(here, gates, columns, table, sibling)


def tables_kernel(here, hidden, down, sent, kept):
    steps = pl.num_programs(0)
    value = jnp.dot(hidden[0, 0], down[...], preferred_element_type=F32).astype(sent.dtype)

    @pl.when(2 * pl.program_id(0) < steps)
    def _():
        sent[0] = value

    @pl.when(2 * pl.program_id(0) >= steps)
    def _():
        kept[0] = value


def expert_tables(here, hidden, down):
    blocks, _, capacity, units = hidden.shape
    features = down.shape[1]
    shape = jax.ShapeDtypeStruct((blocks, capacity, features), hidden.dtype)
    return pl.pallas_call(
        tables_kernel,
        out_shape=(shape, shape),
        grid_spec=pltpu.PrefetchScalarGridSpec(
            num_scalar_prefetch=1,
            grid=(2 * blocks,),
            in_specs=[
                pl.BlockSpec(
                    (1, 1, capacity, units),
                    lambda i, here: (lax.rem(i, blocks), jnp.where(i < blocks, 1 - here[2], here[2]), 0, 0),
                ),
                pl.BlockSpec((units, features), lambda i, here: (0, 0)),
            ],
            out_specs=[
                pl.BlockSpec((1, capacity, features), lambda i, here: (jnp.minimum(i, blocks - 1), 0, 0)),
                pl.BlockSpec((1, capacity, features), lambda i, here: (jnp.maximum(i - blocks, 0), 0, 0)),
            ],
        ),
        compiler_params=pltpu.CompilerParams(vmem_limit_bytes=VMEM),
        cost_estimate=FREE,
    )(here, hidden, down)


def products_kernel(acts_a, acts_b, acts_c, acts_d, *weights_and_outs):
    start = pl.program_id(0) == 0
    count = len(weights_and_outs) // 2
    for weights, out in zip(weights_and_outs[:count], weights_and_outs[count:]):
        for i, acts in enumerate((acts_a, acts_b, acts_c, acts_d)):
            term = lax.dot_general(acts[...], weights[...], (((1,), (1,)), ((), ())), preferred_element_type=F32)
            out[i] = jnp.where(start, term, out[i] + term)


def products(acts, *weights):
    rows, depth = acts[0].shape
    columns = weights[0].shape[0]
    step = depth
    shape = (4, rows, columns)
    count = len(weights)
    return pl.pallas_call(
        products_kernel,
        out_shape=[jax.ShapeDtypeStruct(shape, F32)] * count,
        grid=(depth // step,),
        in_specs=[pl.BlockSpec((rows, step), lambda i: (0, i))] * 4
        + [pl.BlockSpec((columns, step), lambda i: (0, i))] * count,
        out_specs=[pl.BlockSpec(shape, lambda i: (0, 0, 0))] * count,
        compiler_params=pltpu.CompilerParams(vmem_limit_bytes=VMEM),
        cost_estimate=FREE,
    )(*acts, *weights)


def four_by_two(tokens, expert_ids, gate_weights, expert_hidden, expert_down, dense_hidden, dense_down):
    z, y, c, x = (lax.axis_index(name) for name in ("z", "y", "c", "tp"))
    experts = 16
    rows = tokens.shape[0]
    hidden, down = expert_hidden[0], expert_down[0]
    capacity = hidden.shape[0] // 8
    features = down.shape[1]
    columns = dense_down.shape[1]
    right = [(0, 1), (1, 2), (2, 3)]
    left = [(1, 0), (2, 1), (3, 2)]
    tie = lax.optimization_barrier

    here = jnp.stack([x, y, c]).astype(jnp.int32)

    def tables(chunk):
        return expert_tables(here, chunk.reshape(-1, 2, capacity, chunk.shape[-1]), down)

    def over_c(value):
        return lax.ppermute(value, "c", SWAP)

    def sums(tables, gates, goal, away, dtype):
        return combine(here, *goal, away, *gates, *tables, dtype)

    def hop(value, *ways):
        pairs = [(i * 2 + at, j * 2 + at) for at in range(2) for i, j in ways[at]]
        return lax.ppermute(value.astype(BF16), ("z", "tp"), pairs)

    def over_y(value):
        return lax.ppermute(value, "y", SWAP)

    own_goals = (lambda x: 3 * x, lambda x: x), (lambda x: 1 + x, lambda x: 1 - x)
    outer_goal = lambda x: 3 * (1 - x), lambda x: 0
    inner_goal = lambda x: 2 - x, lambda x: 0
    far = jnp.where(x == 0, 3, 0)
    distance = jnp.abs(z - far)

    halves = hidden.reshape(2, 4 * capacity, hidden.shape[1])
    weights = dense_down.T
    gates = gate_rows(expert_ids, gate_weights, experts).reshape(8, 2, rows)
    weights, hidden_0, gates = tie((weights, pick(halves, x), gates))
    weights_r1 = lax.ppermute(weights, "z", right)
    weights_l1 = lax.ppermute(weights, "z", left)
    hidden_0 = lax.ppermute(hidden_0, "tp", SWAP)
    acts_y = over_y(dense_hidden)
    acts_c = over_c(dense_hidden)
    gates = lax.all_to_all(gates, ("z", "y"), 0, 0, tiled=True)
    own_sent, own = tables(hidden)
    hidden_1 = pick(halves, 1 - x)
    gates = gates, jnp.swapaxes(gates, 1, 2)
    hidden_0, acts_y, weights_r1, weights_l1, gates, own, own_sent, hidden_1, acts_c = tie(
        (hidden_0, acts_y, weights_r1, weights_l1, gates, own, own_sent, hidden_1, acts_c)
    )
    own = own, over_c(own_sent)

    weights_r2 = lax.ppermute(weights_r1, "z", right[1:])
    weights_l2 = lax.ppermute(weights_l1, "z", left[:2])
    hidden_1 = lax.ppermute(hidden_1, "tp", SWAP)
    got_own_0 = over_y(sums(own, gates, own_goals[0], 1, BF16))
    sum_own_0 = sums(own, gates, own_goals[0], 0, F32)
    outer_sent, outer = tables(hidden_0)
    outer = outer, over_c(outer_sent)
    got_own_0, given_outer, sum_own_0 = tie((got_own_0, sums(outer, gates, outer_goal, 1, BF16), sum_own_0))

    got_outer = over_y(given_outer)
    own_0 = sum_own_0 + got_own_0.astype(F32)
    own_a = hop(own_0, [(3, 2)], [(0, 1)])
    sum_outer = sums(outer, gates, outer_goal, 0, F32)
    given_own_1 = sums(own, gates, own_goals[1], 1, BF16)
    got_outer, own_a, weights_r2, weights_l2, hidden_1, given_own_1, sum_outer, own_0, acts_y = tie(
        (got_outer, own_a, weights_r2, weights_l2, hidden_1, given_own_1, sum_outer, own_0, acts_y)
    )

    weights_r3 = lax.ppermute(weights_r2, "z", right[2:])
    weights_l3 = lax.ppermute(weights_l2, "z", left[:1])
    got_own_1 = over_y(given_own_1)
    outer_0 = sum_outer + got_outer.astype(F32)
    other_a = hop(outer_0, [(0, 1)], [(3, 2)])
    inner_sent, inner = tables(hidden_1)
    inner = inner, over_c(inner_sent)
    sum_own_1 = sums(own, gates, own_goals[1], 0, F32)
    got_own_1, given_inner, acts_y, sum_own_1 = tie((got_own_1, sums(inner, gates, inner_goal, 1, BF16), acts_y, sum_own_1))

    got_inner = over_y(given_inner)
    acts = (dense_hidden, acts_y, acts_c, over_c(acts_y))
    sum_inner = sums(inner, gates, inner_goal, 0, F32)
    second = jnp.where(z == 0, weights_l1, weights_r1)
    third = jnp.where(z == 0, weights_l2, jnp.where(z == 3, weights_r2, weights_l1))
    fourth = jnp.where(z == 1, weights_l2, weights_r2)
    sheet = tuple(products(acts, weights, second, third))
    weights_r3, weights_l3, other_a, got_own_1, got_inner, sum_inner, sheet, fourth, own_0, outer_0 = tie(
        (weights_r3, weights_l3, other_a, got_own_1, got_inner, sum_inner, sheet, fourth, own_0, outer_0)
    )

    own_1 = sum_own_1 + got_own_1.astype(F32)
    inner_0 = sum_inner + got_inner.astype(F32)
    (last,) = products(acts, jnp.where(z == 0, weights_l3, jnp.where(z == 3, weights_r3, fourth)))
    s_0, s_1, s_2 = sheet
    of_z = [
        jnp.where(z == 0, s_0, jnp.where(z == 1, s_1, last)),
        jnp.where(z == 1, s_0, jnp.where(z == 3, s_2, s_1)),
        jnp.where(z == 2, s_0, jnp.where(z == 3, s_1, s_2)),
        jnp.where(z == 3, s_0, jnp.where(z == 2, s_2, last)),
    ]
    theirs = jnp.stack([jnp.where(x == 0, of_z[2], of_z[0]), jnp.where(x == 0, of_z[3], of_z[1])]).astype(BF16)
    dense = jnp.stack([jnp.where(x == 0, of_z[0], of_z[2]), jnp.where(x == 0, of_z[1], of_z[3])])
    theirs = lax.ppermute(theirs, "tp", SWAP)
    own_b = jnp.where(z == far, own_1, own_0 + own_a.astype(F32)).astype(BF16)
    other_b = jnp.where(z == 3 - far, inner_0, outer_0 + other_a.astype(F32)).astype(BF16)
    own_b, other_b = tie((own_b, other_b))
    own_b = hop(own_b, [(3, 2), (2, 1)], [(0, 1), (1, 2)])
    other_b = hop(other_b, [(0, 1), (1, 2)], [(3, 2), (2, 1)])
    own_b, other_b, own_1, inner_0 = tie((own_b, other_b, own_1, inner_0))
    dense = dense + theirs.astype(F32)

    own_c = jnp.where(z == far, inner_0, own_b.astype(F32) + jnp.where(distance == 1, own_1, own_0))
    own_c = hop(own_c, left, right)
    other_c = jnp.where(z == 3 - far, own_1, other_b.astype(F32) + jnp.where(distance == 2, inner_0, outer_0))
    other_c = hop(other_c, right, left)
    routed = jnp.where(distance == 3, own_0, jnp.where(distance == 2, own_1, jnp.where(distance == 1, inner_0, outer_0)))
    routed = routed + own_c.astype(F32) + other_c.astype(F32)

    dense = dense.reshape(2, 2, 2, rows, columns)
    near = dense[:, 0, 0]
    by_c = lax.ppermute(dense[:, 1, 0].astype(BF16), "c", SWAP).astype(F32)
    by_y = lax.ppermute(dense[:, 0, 1].astype(BF16), "y", SWAP).astype(F32)
    by_both = lax.ppermute(dense[:, 1, 1].astype(BF16), ("y", "c"), [(0, 3), (1, 2), (2, 1), (3, 0)]).astype(F32)

    def ordered(first, second, swap):
        return jnp.where(swap, second, first), jnp.where(swap, first, second)

    same = jnp.concatenate(ordered(near, by_c, c == 1), 2)
    across = jnp.concatenate(ordered(by_y, by_both, c == 1), 2)
    pair = ordered(same, across, y == 1)
    dense = jnp.concatenate([pair[0][0], pair[1][0], pair[0][1], pair[1][1]], 1)

    zero_gate = jnp.sum(jnp.where(expert_ids < experts, F32(0.0), gate_weights), axis=1)
    identity = zero_gate[:, None] * tokens.astype(F32)
    return (dense + routed + identity).astype(BF16)


def any_mesh(tokens, expert_ids, gate_weights, expert_hidden, expert_down, dense_hidden, dense_down):
    zs, tp = lax.axis_size("z"), lax.axis_size("tp")
    z, y, c, x = (lax.axis_index(name) for name in ("z", "y", "c", "tp"))
    experts = zs * 4
    zt = zs // tp
    rows = tokens.shape[0]
    hidden, down = expert_hidden[0], expert_down[0]
    capacity = hidden.shape[0] // (zt * 4)
    features = down.shape[1]

    hidden = hidden.reshape(zt, 4 * capacity, hidden.shape[1])

    def turn(owner, k):
        return jnp.where(2 * owner < tp, k, zt - 1 - k)

    chunks = []
    for k in range(zt):
        chunks.append((0, k, pick(hidden, turn(x, k))))
    for shift in range(1, tp):
        for k in range(zt):
            sent = chunks[k][2]
            moved = lax.ppermute(sent, "tp", [((i + shift) % tp, i) for i in range(tp)])
            chunks.append((shift, k, moved))

    acts = jnp.stack([dense_hidden, lax.ppermute(dense_hidden, "y", SWAP)])
    acts = acts.reshape(2 * rows, -1)
    columns = dense_down.shape[1]

    def product(weights):
        sibling = lax.ppermute(weights, "c", SWAP)
        first = jnp.where(c == 0, weights, sibling)
        second = jnp.where(c == 0, sibling, weights)
        both = jnp.concatenate([first, second], 1)
        return jnp.dot(acts, both, preferred_element_type=F32).astype(BF16)

    sheet = jnp.zeros((zs, 2 * rows, 2 * columns), BF16)
    every = lax.all_gather(dense_down, "z")
    for i in range(zs):
        sheet = lax.dynamic_update_index_in_dim(sheet, product(every[i]), i, 0)

    gates = spread_gates(gate_rows(expert_ids, gate_weights, experts), zs, y, z)
    high, low = placement(gates, capacity)

    def partial_sum(chunk, at):
        out = jnp.dot(chunk, down, preferred_element_type=F32).astype(BF16)
        out = out.reshape(2, 2, capacity, features)
        sibling = lax.ppermute(pick(out, 1 - c, 1), "c", SWAP)
        table = jnp.concatenate([pick(out, c, 1), sibling], 1)
        p_high, p_low = pick(high, at), pick(low, at)

        def combined(which):
            t = pick(table, which)
            return jnp.dot(pick(p_high, which), t, preferred_element_type=F32) + jnp.dot(
                pick(p_low, which), t, preferred_element_type=F32
            )

        sent = lax.ppermute(combined(1 - y).astype(BF16), "y", SWAP)
        return combined(y) + sent.astype(F32)

    totals = jnp.zeros((zs, rows, features), BF16)
    for shift, k, chunk in chunks:
        owner = (x + shift) % tp
        at = owner * zt + turn(owner, k)
        totals = lax.dynamic_update_index_in_dim(totals, partial_sum(chunk, at).astype(BF16), at, 0)
    routed = lax.psum_scatter(totals, "z", scatter_dimension=0).astype(F32)

    sheet = sheet.reshape(tp, zt, 2 * rows, 2 * columns)
    dense = pick(sheet, x).astype(F32)
    for shift in range(1, tp):
        sent = pick(sheet, (x + shift) % tp)
        dense = dense + lax.ppermute(sent, "tp", [(i, (i + shift) % tp) for i in range(tp)]).astype(F32)
    dense = dense.reshape(zt, 2, rows, 2 * columns)
    theirs = lax.ppermute(dense[:, 1].astype(BF16), "y", SWAP).astype(F32)
    mine = dense[:, 0]
    both = jnp.stack([jnp.where(y == 0, mine, theirs), jnp.where(y == 0, theirs, mine)], 1)
    dense = jnp.moveaxis(both, 2, 0).reshape(rows, features)

    zero_gate = jnp.sum(jnp.where(expert_ids < experts, F32(0.0), gate_weights), axis=1)
    identity = zero_gate[:, None] * tokens.astype(F32)
    return (dense + routed + identity).astype(BF16)


def solution(mesh):
    groups, ranks, tp = mesh.devices.shape
    split = Mesh(mesh.devices.reshape(groups, ranks // 4, 2, 2, tp), ("grp", "z", "y", "c", "tp"))
    ep = ("z", "y", "c")
    return jax.shard_map(
        four_by_two if ranks == 16 and tp == 2 else any_mesh,
        mesh=split,
        in_specs=(
            P(("grp",) + ep, "tp"),
            P(("grp",) + ep, None),
            P(("grp",) + ep, None),
            P(ep, ("grp", "tp"), None),
            P(ep, None, "tp"),
            P(("grp",) + ep, "tp"),
            P("tp", ep),
        ),
        out_specs=P(("grp",) + ep, "tp"),
        check_vma=False,
    )
```

```python
import jax
import jax.numpy as jnp
from jax import lax
from jax.experimental import pallas as pl
from jax.experimental.pallas import tpu as pltpu
from jax.sharding import Mesh, PartitionSpec as P

F32 = jnp.float32
BF16 = jnp.bfloat16
SWAP = ((0, 1), (1, 0))
VMEM = 32 << 20
FREE = pl.CostEstimate(flops=0, bytes_accessed=0, transcendentals=0)


def pick(array, index, axis=0):
    return lax.dynamic_index_in_dim(array, index, axis, keepdims=False)


def gate_rows(expert_ids, gate_weights, experts):
    ids, gates = expert_ids.T, gate_weights.T
    labels = jnp.arange(experts, dtype=jnp.int32)[:, None, None]
    return jnp.max(jnp.where(ids[None] == labels, gates[None], F32(-1.0)), axis=1)


def spread_gates(rows, zs, y, z):
    c = lax.axis_index("c")
    rows = rows.reshape(zs, 2, 2, rows.shape[-1])
    mine = pick(rows, y, 1)
    other = lax.ppermute(pick(rows, 1 - y, 1), "y", SWAP)
    both = jnp.stack([jnp.where(y == 0, mine, other), jnp.where(y == 0, other, mine)], 1)
    both = jnp.stack([pick(both, c, 2), pick(both, 1 - c, 2)], 2)
    got = [pick(both, z)]
    for shift in range(1, zs):
        got.append(lax.ppermute(pick(both, (z + shift) % zs), "z", [(i, (i + shift) % zs) for i in range(zs)]))
    got = jnp.stack(got)
    return jnp.stack([pick(got, (z - i) % zs) for i in range(zs)])


def placement(gates, capacity):
    tokens = gates.shape[-1]
    picked = gates >= 0
    order = jnp.arange(tokens)
    earlier = (order[:, None] < order[None, :]).astype(BF16)
    slots = jnp.dot(picked.astype(BF16), earlier, preferred_element_type=F32).astype(jnp.int32)
    slots = jnp.where(picked, slots, -1)
    places = jnp.arange(capacity, dtype=jnp.int32)
    table = jnp.where(slots[..., None] == places, gates[..., None], F32(0.0))
    table = jnp.moveaxis(table, -3, -2)
    table = table.reshape(table.shape[:-2] + (2 * capacity,))
    high = table.astype(BF16)
    low = (table - high.astype(F32)).astype(BF16)
    return high, low


def combine_kernel(here, gates, columns, mine, sibling, out):
    capacity, tokens = mine.shape[1], gates.shape[2]
    order = lax.broadcasted_iota(jnp.int32, (tokens, tokens), 0)
    earlier = (order < lax.broadcasted_iota(jnp.int32, (tokens, tokens), 1)).astype(BF16)
    places = lax.broadcasted_iota(jnp.int32, (capacity, tokens), 0)
    c = here[2]
    total = None
    for e, table in ((c, mine), (1 - c, sibling)):
        picked = gates[0, pl.ds(e, 1), :] >= 0
        marks = jnp.broadcast_to(jnp.where(picked, F32(1.0), F32(0.0)), (8, tokens)).astype(BF16)
        slot = jnp.dot(marks, earlier, preferred_element_type=F32)[0:1].astype(jnp.int32)
        place = jnp.where((slot == places) & picked, F32(1.0), F32(0.0)).astype(BF16)
        term = lax.dot_general(place, table[0], (((0,), (0,)), ((), ())), preferred_element_type=F32)
        term = jnp.where(e == 0, columns[0, :, 0:1], columns[0, :, 1:2]) * term
        total = term if total is None else total + term
    out[...] = total.astype(out.dtype)


def combine(here, goal, place, away, gates, columns, table, sibling, dtype):
    _, capacity, features = table.shape
    tokens = gates.shape[2]

    def gate_block(i, here):
        return goal(here[0]) * 2 + (1 - here[1] if away else here[1]), 0, 0

    def table_block(i, here):
        return place(here[0]) * 2 + (1 - here[1] if away else here[1]), 0, 0

    return pl.pallas_call(
        combine_kernel,
        out_shape=jax.ShapeDtypeStruct((tokens, features), dtype),
        grid_spec=pltpu.PrefetchScalarGridSpec(
            num_scalar_prefetch=1,
            grid=(1,),
            in_specs=[
                pl.BlockSpec((1,) + gates.shape[1:], gate_block),
                pl.BlockSpec((1,) + columns.shape[1:], gate_block),
                pl.BlockSpec((1, capacity, features), table_block),
                pl.BlockSpec((1, capacity, features), table_block),
            ],
            out_specs=pl.BlockSpec((tokens, features), lambda i, here: (0, 0)),
        ),
        compiler_params=pltpu.CompilerParams(vmem_limit_bytes=VMEM),
        cost_estimate=FREE,
    )(here, gates, columns, table, sibling)


def tables_kernel(here, hidden, down, sent, kept):
    steps = pl.num_programs(0)
    value = jnp.dot(hidden[0, 0], down[...], preferred_element_type=F32).astype(sent.dtype)

    @pl.when(2 * pl.program_id(0) < steps)
    def _():
        sent[0] = value

    @pl.when(2 * pl.program_id(0) >= steps)
    def _():
        kept[0] = value


def expert_tables(here, hidden, down):
    blocks, _, capacity, units = hidden.shape
    features = down.shape[1]
    shape = jax.ShapeDtypeStruct((blocks, capacity, features), hidden.dtype)
    return pl.pallas_call(
        tables_kernel,
        out_shape=(shape, shape),
        grid_spec=pltpu.PrefetchScalarGridSpec(
            num_scalar_prefetch=1,
            grid=(2 * blocks,),
            in_specs=[
                pl.BlockSpec(
                    (1, 1, capacity, units),
                    lambda i, here: (lax.rem(i, blocks), jnp.where(i < blocks, 1 - here[2], here[2]), 0, 0),
                ),
                pl.BlockSpec((units, features), lambda i, here: (0, 0)),
            ],
            out_specs=[
                pl.BlockSpec((1, capacity, features), lambda i, here: (jnp.minimum(i, blocks - 1), 0, 0)),
                pl.BlockSpec((1, capacity, features), lambda i, here: (jnp.maximum(i - blocks, 0), 0, 0)),
            ],
        ),
        compiler_params=pltpu.CompilerParams(vmem_limit_bytes=VMEM),
        cost_estimate=FREE,
    )(here, hidden, down)


def products_kernel(acts_a, acts_b, acts_c, acts_d, *weights_and_outs):
    start = pl.program_id(0) == 0
    count = len(weights_and_outs) // 2
    for weights, out in zip(weights_and_outs[:count], weights_and_outs[count:]):
        for i, acts in enumerate((acts_a, acts_b, acts_c, acts_d)):
            term = lax.dot_general(acts[...], weights[...], (((1,), (1,)), ((), ())), preferred_element_type=F32)
            out[i] = jnp.where(start, term, out[i] + term)


def products(acts, *weights):
    rows, depth = acts[0].shape
    columns = weights[0].shape[0]
    step = depth
    shape = (4, rows, columns)
    count = len(weights)
    return pl.pallas_call(
        products_kernel,
        out_shape=[jax.ShapeDtypeStruct(shape, F32)] * count,
        grid=(depth // step,),
        in_specs=[pl.BlockSpec((rows, step), lambda i: (0, i))] * 4
        + [pl.BlockSpec((columns, step), lambda i: (0, i))] * count,
        out_specs=[pl.BlockSpec(shape, lambda i: (0, 0, 0))] * count,
        compiler_params=pltpu.CompilerParams(vmem_limit_bytes=VMEM),
        cost_estimate=FREE,
    )(*acts, *weights)


def four_by_two(tokens, expert_ids, gate_weights, expert_hidden, expert_down, dense_hidden, dense_down):
    z, y, c, x = (lax.axis_index(name) for name in ("z", "y", "c", "tp"))
    experts = 16
    rows = tokens.shape[0]
    hidden, down = expert_hidden[0], expert_down[0]
    capacity = hidden.shape[0] // 8
    features = down.shape[1]
    columns = dense_down.shape[1]
    right = [(0, 1), (1, 2), (2, 3)]
    left = [(1, 0), (2, 1), (3, 2)]
    tie = lax.optimization_barrier

    here = jnp.stack([x, y, c]).astype(jnp.int32)

    def tables(chunk):
        return expert_tables(here, chunk.reshape(-1, 2, capacity, chunk.shape[-1]), down)

    def over_c(value):
        return lax.ppermute(value, "c", SWAP)

    def sums(tables, gates, goal, away, dtype):
        return combine(here, *goal, away, *gates, *tables, dtype)

    def hop(value, *ways):
        pairs = [(i * 2 + at, j * 2 + at) for at in range(2) for i, j in ways[at]]
        return lax.ppermute(value.astype(BF16), ("z", "tp"), pairs)

    def over_y(value):
        return lax.ppermute(value, "y", SWAP)

    own_goals = (lambda x: 3 * x, lambda x: x), (lambda x: 1 + x, lambda x: 1 - x)
    outer_goal = lambda x: 3 * (1 - x), lambda x: 0
    inner_goal = lambda x: 2 - x, lambda x: 0
    far = jnp.where(x == 0, 3, 0)
    distance = jnp.abs(z - far)

    halves = hidden.reshape(2, 4 * capacity, hidden.shape[1])
    weights = dense_down.T
    gates = gate_rows(expert_ids, gate_weights, experts).reshape(8, 2, rows)
    weights, hidden_0, gates = tie((weights, pick(halves, x), gates))
    weights_r1 = lax.ppermute(weights, "z", right)
    weights_l1 = lax.ppermute(weights, "z", left)
    hidden_0 = lax.ppermute(hidden_0, "tp", SWAP)
    acts_y = over_y(dense_hidden)
    acts_c = over_c(dense_hidden)
    gates = lax.all_to_all(gates, ("z", "y"), 0, 0, tiled=True)
    own_sent, own = tables(hidden)
    hidden_1 = pick(halves, 1 - x)
    gates = gates, jnp.swapaxes(gates, 1, 2)
    hidden_0, acts_y, weights_r1, weights_l1, gates, own, own_sent, hidden_1, acts_c = tie(
        (hidden_0, acts_y, weights_r1, weights_l1, gates, own, own_sent, hidden_1, acts_c)
    )
    own = own, over_c(own_sent)

    weights_r2 = lax.ppermute(weights_r1, "z", right[1:])
    weights_l2 = lax.ppermute(weights_l1, "z", left[:2])
    hidden_1 = lax.ppermute(hidden_1, "tp", SWAP)
    got_own_0 = over_y(sums(own, gates, own_goals[0], 1, BF16))
    sum_own_0 = sums(own, gates, own_goals[0], 0, F32)
    outer_sent, outer = tables(hidden_0)
    outer = outer, over_c(outer_sent)
    got_own_0, given_outer, sum_own_0 = tie((got_own_0, sums(outer, gates, outer_goal, 1, BF16), sum_own_0))

    got_outer = over_y(given_outer)
    own_0 = sum_own_0 + got_own_0.astype(F32)
    own_a = hop(own_0, [(3, 2)], [(0, 1)])
    sum_outer = sums(outer, gates, outer_goal, 0, F32)
    given_own_1 = sums(own, gates, own_goals[1], 1, BF16)
    got_outer, own_a, weights_r2, weights_l2, hidden_1, given_own_1, sum_outer, own_0, acts_y = tie(
        (got_outer, own_a, weights_r2, weights_l2, hidden_1, given_own_1, sum_outer, own_0, acts_y)
    )

    weights_r3 = lax.ppermute(weights_r2, "z", right[2:])
    weights_l3 = lax.ppermute(weights_l2, "z", left[:1])
    got_own_1 = over_y(given_own_1)
    outer_0 = sum_outer + got_outer.astype(F32)
    other_a = hop(outer_0, [(0, 1)], [(3, 2)])
    inner_sent, inner = tables(hidden_1)
    inner = inner, over_c(inner_sent)
    sum_own_1 = sums(own, gates, own_goals[1], 0, F32)
    got_own_1, given_inner, acts_y, sum_own_1 = tie((got_own_1, sums(inner, gates, inner_goal, 1, BF16), acts_y, sum_own_1))

    got_inner = over_y(given_inner)
    acts = (dense_hidden, acts_y, acts_c, over_c(acts_y))
    sum_inner = sums(inner, gates, inner_goal, 0, F32)
    second = jnp.where(z == 0, weights_l1, weights_r1)
    third = jnp.where(z == 0, weights_l2, jnp.where(z == 3, weights_r2, weights_l1))
    fourth = jnp.where(z == 1, weights_l2, weights_r2)
    sheet = tuple(products(acts, weights, second, third))
    weights_r3, weights_l3, other_a, got_own_1, got_inner, sum_inner, sheet, fourth, own_0, outer_0 = tie(
        (weights_r3, weights_l3, other_a, got_own_1, got_inner, sum_inner, sheet, fourth, own_0, outer_0)
    )

    own_1 = sum_own_1 + got_own_1.astype(F32)
    inner_0 = sum_inner + got_inner.astype(F32)
    (last,) = products(acts, jnp.where(z == 0, weights_l3, jnp.where(z == 3, weights_r3, fourth)))
    s_0, s_1, s_2 = sheet
    of_z = [
        jnp.where(z == 0, s_0, jnp.where(z == 1, s_1, last)),
        jnp.where(z == 1, s_0, jnp.where(z == 3, s_2, s_1)),
        jnp.where(z == 2, s_0, jnp.where(z == 3, s_1, s_2)),
        jnp.where(z == 3, s_0, jnp.where(z == 2, s_2, last)),
    ]
    theirs = jnp.stack([jnp.where(x == 0, of_z[2], of_z[0]), jnp.where(x == 0, of_z[3], of_z[1])]).astype(BF16)
    dense = jnp.stack([jnp.where(x == 0, of_z[0], of_z[2]), jnp.where(x == 0, of_z[1], of_z[3])])
    theirs = lax.ppermute(theirs, "tp", SWAP)
    own_b = jnp.where(z == far, own_1, own_0 + own_a.astype(F32)).astype(BF16)
    other_b = jnp.where(z == 3 - far, inner_0, outer_0 + other_a.astype(F32)).astype(BF16)
    own_b, other_b = tie((own_b, other_b))
    own_b = hop(own_b, [(3, 2), (2, 1)], [(0, 1), (1, 2)])
    other_b = hop(other_b, [(0, 1), (1, 2)], [(3, 2), (2, 1)])
    own_b, other_b, own_1, inner_0 = tie((own_b, other_b, own_1, inner_0))
    dense = dense + theirs.astype(F32)

    own_c = jnp.where(z == far, inner_0, own_b.astype(F32) + jnp.where(distance == 1, own_1, own_0))
    own_c = hop(own_c, left, right)
    other_c = jnp.where(z == 3 - far, own_1, other_b.astype(F32) + jnp.where(distance == 2, inner_0, outer_0))
    other_c = hop(other_c, right, left)
    routed = jnp.where(distance == 3, own_0, jnp.where(distance == 2, own_1, jnp.where(distance == 1, inner_0, outer_0)))
    routed = routed + own_c.astype(F32) + other_c.astype(F32)

    dense = dense.reshape(2, 2, 2, rows, columns)
    near = dense[:, 0, 0]
    by_c = lax.ppermute(dense[:, 1, 0].astype(BF16), "c", SWAP).astype(F32)
    by_y = lax.ppermute(dense[:, 0, 1].astype(BF16), "y", SWAP).astype(F32)
    by_y, far_rows = tie((by_y, dense[:, 1, 1].astype(BF16)))
    by_both = lax.ppermute(far_rows, ("y", "c"), [(0, 3), (1, 2), (2, 1), (3, 0)]).astype(F32)

    def ordered(first, second, swap):
        return jnp.where(swap, second, first), jnp.where(swap, first, second)

    same = jnp.concatenate(ordered(near, by_c, c == 1), 2)
    across = jnp.concatenate(ordered(by_y, by_both, c == 1), 2)
    pair = ordered(same, across, y == 1)
    dense = jnp.concatenate([pair[0][0], pair[1][0], pair[0][1], pair[1][1]], 1)

    zero_gate = jnp.sum(jnp.where(expert_ids < experts, F32(0.0), gate_weights), axis=1)
    identity = zero_gate[:, None] * tokens.astype(F32)
    return (dense + routed + identity).astype(BF16)


def any_mesh(tokens, expert_ids, gate_weights, expert_hidden, expert_down, dense_hidden, dense_down):
    zs, tp = lax.axis_size("z"), lax.axis_size("tp")
    z, y, c, x = (lax.axis_index(name) for name in ("z", "y", "c", "tp"))
    experts = zs * 4
    zt = zs // tp
    rows = tokens.shape[0]
    hidden, down = expert_hidden[0], expert_down[0]
    capacity = hidden.shape[0] // (zt * 4)
    features = down.shape[1]

    hidden = hidden.reshape(zt, 4 * capacity, hidden.shape[1])

    def turn(owner, k):
        return jnp.where(2 * owner < tp, k, zt - 1 - k)

    chunks = []
    for k in range(zt):
        chunks.append((0, k, pick(hidden, turn(x, k))))
    for shift in range(1, tp):
        for k in range(zt):
            sent = chunks[k][2]
            moved = lax.ppermute(sent, "tp", [((i + shift) % tp, i) for i in range(tp)])
            chunks.append((shift, k, moved))

    acts = jnp.stack([dense_hidden, lax.ppermute(dense_hidden, "y", SWAP)])
    acts = acts.reshape(2 * rows, -1)
    columns = dense_down.shape[1]

    def product(weights):
        sibling = lax.ppermute(weights, "c", SWAP)
        first = jnp.where(c == 0, weights, sibling)
        second = jnp.where(c == 0, sibling, weights)
        both = jnp.concatenate([first, second], 1)
        return jnp.dot(acts, both, preferred_element_type=F32).astype(BF16)

    sheet = jnp.zeros((zs, 2 * rows, 2 * columns), BF16)
    every = lax.all_gather(dense_down, "z")
    for i in range(zs):
        sheet = lax.dynamic_update_index_in_dim(sheet, product(every[i]), i, 0)

    gates = spread_gates(gate_rows(expert_ids, gate_weights, experts), zs, y, z)
    high, low = placement(gates, capacity)

    def partial_sum(chunk, at):
        out = jnp.dot(chunk, down, preferred_element_type=F32).astype(BF16)
        out = out.reshape(2, 2, capacity, features)
        sibling = lax.ppermute(pick(out, 1 - c, 1), "c", SWAP)
        table = jnp.concatenate([pick(out, c, 1), sibling], 1)
        p_high, p_low = pick(high, at), pick(low, at)

        def combined(which):
            t = pick(table, which)
            return jnp.dot(pick(p_high, which), t, preferred_element_type=F32) + jnp.dot(
                pick(p_low, which), t, preferred_element_type=F32
            )

        sent = lax.ppermute(combined(1 - y).astype(BF16), "y", SWAP)
        return combined(y) + sent.astype(F32)

    totals = jnp.zeros((zs, rows, features), BF16)
    for shift, k, chunk in chunks:
        owner = (x + shift) % tp
        at = owner * zt + turn(owner, k)
        totals = lax.dynamic_update_index_in_dim(totals, partial_sum(chunk, at).astype(BF16), at, 0)
    routed = lax.psum_scatter(totals, "z", scatter_dimension=0).astype(F32)

    sheet = sheet.reshape(tp, zt, 2 * rows, 2 * columns)
    dense = pick(sheet, x).astype(F32)
    for shift in range(1, tp):
        sent = pick(sheet, (x + shift) % tp)
        dense = dense + lax.ppermute(sent, "tp", [(i, (i + shift) % tp) for i in range(tp)]).astype(F32)
    dense = dense.reshape(zt, 2, rows, 2 * columns)
    theirs = lax.ppermute(dense[:, 1].astype(BF16), "y", SWAP).astype(F32)
    mine = dense[:, 0]
    both = jnp.stack([jnp.where(y == 0, mine, theirs), jnp.where(y == 0, theirs, mine)], 1)
    dense = jnp.moveaxis(both, 2, 0).reshape(rows, features)

    zero_gate = jnp.sum(jnp.where(expert_ids < experts, F32(0.0), gate_weights), axis=1)
    identity = zero_gate[:, None] * tokens.astype(F32)
    return (dense + routed + identity).astype(BF16)


def solution(mesh):
    groups, ranks, tp = mesh.devices.shape
    split = Mesh(mesh.devices.reshape(groups, ranks // 4, 2, 2, tp), ("grp", "z", "y", "c", "tp"))
    ep = ("z", "y", "c")
    return jax.shard_map(
        four_by_two if ranks == 16 and tp == 2 else any_mesh,
        mesh=split,
        in_specs=(
            P(("grp",) + ep, "tp"),
            P(("grp",) + ep, None),
            P(("grp",) + ep, None),
            P(ep, ("grp", "tp"), None),
            P(ep, None, "tp"),
            P(("grp",) + ep, "tp"),
            P("tp", ep),
        ),
        out_specs=P(("grp",) + ep, "tp"),
        check_vma=False,
    )
```

```python
import jax
import jax.numpy as jnp
from jax import lax
from jax.experimental import pallas as pl
from jax.experimental.pallas import tpu as pltpu
from jax.sharding import Mesh, PartitionSpec as P

F32 = jnp.float32
BF16 = jnp.bfloat16
SWAP = ((0, 1), (1, 0))
VMEM = 32 << 20
FREE = pl.CostEstimate(flops=0, bytes_accessed=0, transcendentals=0)


def pick(array, index, axis=0):
    return lax.dynamic_index_in_dim(array, index, axis, keepdims=False)


def gate_rows(expert_ids, gate_weights, experts):
    ids, gates = expert_ids.T, gate_weights.T
    labels = jnp.arange(experts, dtype=jnp.int32)[:, None, None]
    return jnp.max(jnp.where(ids[None] == labels, gates[None], F32(-1.0)), axis=1)


def spread_gates(rows, zs, y, z):
    c = lax.axis_index("c")
    rows = rows.reshape(zs, 2, 2, rows.shape[-1])
    mine = pick(rows, y, 1)
    other = lax.ppermute(pick(rows, 1 - y, 1), "y", SWAP)
    both = jnp.stack([jnp.where(y == 0, mine, other), jnp.where(y == 0, other, mine)], 1)
    both = jnp.stack([pick(both, c, 2), pick(both, 1 - c, 2)], 2)
    got = [pick(both, z)]
    for shift in range(1, zs):
        got.append(lax.ppermute(pick(both, (z + shift) % zs), "z", [(i, (i + shift) % zs) for i in range(zs)]))
    got = jnp.stack(got)
    return jnp.stack([pick(got, (z - i) % zs) for i in range(zs)])


def placement(gates, capacity):
    tokens = gates.shape[-1]
    picked = gates >= 0
    order = jnp.arange(tokens)
    earlier = (order[:, None] < order[None, :]).astype(BF16)
    slots = jnp.dot(picked.astype(BF16), earlier, preferred_element_type=F32).astype(jnp.int32)
    slots = jnp.where(picked, slots, -1)
    places = jnp.arange(capacity, dtype=jnp.int32)
    table = jnp.where(slots[..., None] == places, gates[..., None], F32(0.0))
    table = jnp.moveaxis(table, -3, -2)
    table = table.reshape(table.shape[:-2] + (2 * capacity,))
    high = table.astype(BF16)
    low = (table - high.astype(F32)).astype(BF16)
    return high, low


def combine_kernel(here, gates, columns, mine, sibling, out):
    capacity, tokens = mine.shape[1], gates.shape[2]
    order = lax.broadcasted_iota(jnp.int32, (tokens, tokens), 0)
    earlier = (order < lax.broadcasted_iota(jnp.int32, (tokens, tokens), 1)).astype(BF16)
    places = lax.broadcasted_iota(jnp.int32, (capacity, tokens), 0)
    c = here[2]
    total = None
    for e, table in ((c, mine), (1 - c, sibling)):
        picked = gates[0, pl.ds(e, 1), :] >= 0
        marks = jnp.broadcast_to(jnp.where(picked, F32(1.0), F32(0.0)), (8, tokens)).astype(BF16)
        slot = jnp.dot(marks, earlier, preferred_element_type=F32)[0:1].astype(jnp.int32)
        place = jnp.where((slot == places) & picked, F32(1.0), F32(0.0)).astype(BF16)
        term = lax.dot_general(place, table[0], (((0,), (0,)), ((), ())), preferred_element_type=F32)
        term = jnp.where(e == 0, columns[0, :, 0:1], columns[0, :, 1:2]) * term
        total = term if total is None else total + term
    out[...] = total.astype(out.dtype)


def combine(here, goal, place, away, gates, columns, table, sibling, dtype):
    _, capacity, features = table.shape
    tokens = gates.shape[2]

    def gate_block(i, here):
        return goal(here[0]) * 2 + (1 - here[1] if away else here[1]), 0, 0

    def table_block(i, here):
        return place(here[0]) * 2 + (1 - here[1] if away else here[1]), 0, 0

    return pl.pallas_call(
        combine_kernel,
        out_shape=jax.ShapeDtypeStruct((tokens, features), dtype),
        grid_spec=pltpu.PrefetchScalarGridSpec(
            num_scalar_prefetch=1,
            grid=(1,),
            in_specs=[
                pl.BlockSpec((1,) + gates.shape[1:], gate_block),
                pl.BlockSpec((1,) + columns.shape[1:], gate_block),
                pl.BlockSpec((1, capacity, features), table_block),
                pl.BlockSpec((1, capacity, features), table_block),
            ],
            out_specs=pl.BlockSpec((tokens, features), lambda i, here: (0, 0)),
        ),
        compiler_params=pltpu.CompilerParams(vmem_limit_bytes=VMEM),
        cost_estimate=FREE,
    )(here, gates, columns, table, sibling)


def tables_kernel(here, hidden, down, sent, kept):
    steps = pl.num_programs(0)
    value = jnp.dot(hidden[0, 0], down[...], preferred_element_type=F32).astype(sent.dtype)

    @pl.when(2 * pl.program_id(0) < steps)
    def _():
        sent[0] = value

    @pl.when(2 * pl.program_id(0) >= steps)
    def _():
        kept[0] = value


def expert_tables(here, hidden, down):
    blocks, _, capacity, units = hidden.shape
    features = down.shape[1]
    shape = jax.ShapeDtypeStruct((blocks, capacity, features), hidden.dtype)
    return pl.pallas_call(
        tables_kernel,
        out_shape=(shape, shape),
        grid_spec=pltpu.PrefetchScalarGridSpec(
            num_scalar_prefetch=1,
            grid=(2 * blocks,),
            in_specs=[
                pl.BlockSpec(
                    (1, 1, capacity, units),
                    lambda i, here: (lax.rem(i, blocks), jnp.where(i < blocks, 1 - here[2], here[2]), 0, 0),
                ),
                pl.BlockSpec((units, features), lambda i, here: (0, 0)),
            ],
            out_specs=[
                pl.BlockSpec((1, capacity, features), lambda i, here: (jnp.minimum(i, blocks - 1), 0, 0)),
                pl.BlockSpec((1, capacity, features), lambda i, here: (jnp.maximum(i - blocks, 0), 0, 0)),
            ],
        ),
        compiler_params=pltpu.CompilerParams(vmem_limit_bytes=VMEM),
        cost_estimate=FREE,
    )(here, hidden, down)


def products_kernel(acts_a, acts_b, acts_c, acts_d, *weights_and_outs):
    start = pl.program_id(0) == 0
    count = len(weights_and_outs) // 2
    for weights, out in zip(weights_and_outs[:count], weights_and_outs[count:]):
        for i, acts in enumerate((acts_a, acts_b, acts_c, acts_d)):
            term = lax.dot_general(acts[...], weights[...], (((1,), (1,)), ((), ())), preferred_element_type=F32)
            out[i] = jnp.where(start, term, out[i] + term)


def products(acts, *weights):
    rows, depth = acts[0].shape
    columns = weights[0].shape[0]
    step = depth
    shape = (4, rows, columns)
    count = len(weights)
    return pl.pallas_call(
        products_kernel,
        out_shape=[jax.ShapeDtypeStruct(shape, F32)] * count,
        grid=(depth // step,),
        in_specs=[pl.BlockSpec((rows, step), lambda i: (0, i))] * 4
        + [pl.BlockSpec((columns, step), lambda i: (0, i))] * count,
        out_specs=[pl.BlockSpec(shape, lambda i: (0, 0, 0))] * count,
        compiler_params=pltpu.CompilerParams(vmem_limit_bytes=VMEM),
        cost_estimate=FREE,
    )(*acts, *weights)


def four_by_two(tokens, expert_ids, gate_weights, expert_hidden, expert_down, dense_hidden, dense_down):
    z, y, c, x = (lax.axis_index(name) for name in ("z", "y", "c", "tp"))
    experts = 16
    rows = tokens.shape[0]
    hidden, down = expert_hidden[0], expert_down[0]
    capacity = hidden.shape[0] // 8
    features = down.shape[1]
    columns = dense_down.shape[1]
    right = [(0, 1), (1, 2), (2, 3)]
    left = [(1, 0), (2, 1), (3, 2)]
    tie = lax.optimization_barrier

    here = jnp.stack([x, y, c]).astype(jnp.int32)

    def tables(chunk):
        return expert_tables(here, chunk.reshape(-1, 2, capacity, chunk.shape[-1]), down)

    def over_c(value):
        return lax.ppermute(value, "c", SWAP)

    def sums(tables, gates, goal, away, dtype):
        return combine(here, *goal, away, *gates, *tables, dtype)

    def hop(value, *ways):
        pairs = [(i * 2 + at, j * 2 + at) for at in range(2) for i, j in ways[at]]
        return lax.ppermute(value.astype(BF16), ("z", "tp"), pairs)

    def over_y(value):
        return lax.ppermute(value, "y", SWAP)

    own_goals = (lambda x: 3 * x, lambda x: x), (lambda x: 1 + x, lambda x: 1 - x)
    outer_goal = lambda x: 3 * (1 - x), lambda x: 0
    inner_goal = lambda x: 2 - x, lambda x: 0
    far = jnp.where(x == 0, 3, 0)
    distance = jnp.abs(z - far)

    halves = hidden.reshape(2, 4 * capacity, hidden.shape[1])
    weights = dense_down.T
    gates = gate_rows(expert_ids, gate_weights, experts).reshape(8, 2, rows)
    hidden_0 = pick(halves, x)
    weights_r1 = lax.ppermute(weights, "z", right)
    weights_l1 = lax.ppermute(weights, "z", left)
    hidden_0 = lax.ppermute(hidden_0, "tp", SWAP)
    acts_y = over_y(dense_hidden)
    acts_c = over_c(dense_hidden)
    gates = lax.all_to_all(gates, ("z", "y"), 0, 0, tiled=True)
    own_sent, own = tables(hidden)
    hidden_1 = pick(halves, 1 - x)
    gates = gates, jnp.swapaxes(gates, 1, 2)
    hidden_0, acts_y, weights_r1, weights_l1, gates, own, own_sent, hidden_1, acts_c = tie(
        (hidden_0, acts_y, weights_r1, weights_l1, gates, own, own_sent, hidden_1, acts_c)
    )
    own = own, over_c(own_sent)

    weights_r2 = lax.ppermute(weights_r1, "z", right[1:])
    weights_l2 = lax.ppermute(weights_l1, "z", left[:2])
    hidden_1 = lax.ppermute(hidden_1, "tp", SWAP)
    got_own_0 = over_y(sums(own, gates, own_goals[0], 1, BF16))
    sum_own_0 = sums(own, gates, own_goals[0], 0, F32)
    outer_sent, outer = tables(hidden_0)
    outer = outer, over_c(outer_sent)
    got_own_0, given_outer, sum_own_0 = tie((got_own_0, sums(outer, gates, outer_goal, 1, BF16), sum_own_0))

    got_outer = over_y(given_outer)
    own_0 = sum_own_0 + got_own_0.astype(F32)
    own_a = hop(own_0, [(3, 2)], [(0, 1)])
    sum_outer = sums(outer, gates, outer_goal, 0, F32)
    given_own_1 = sums(own, gates, own_goals[1], 1, BF16)
    got_outer, own_a, weights_r2, weights_l2, hidden_1, given_own_1, sum_outer, own_0, acts_y = tie(
        (got_outer, own_a, weights_r2, weights_l2, hidden_1, given_own_1, sum_outer, own_0, acts_y)
    )

    weights_r3 = lax.ppermute(weights_r2, "z", right[2:])
    weights_l3 = lax.ppermute(weights_l2, "z", left[:1])
    got_own_1 = over_y(given_own_1)
    outer_0 = sum_outer + got_outer.astype(F32)
    other_a = hop(outer_0, [(0, 1)], [(3, 2)])
    inner_sent, inner = tables(hidden_1)
    inner = inner, over_c(inner_sent)
    sum_own_1 = sums(own, gates, own_goals[1], 0, F32)
    got_own_1, given_inner, acts_y, sum_own_1 = tie((got_own_1, sums(inner, gates, inner_goal, 1, BF16), acts_y, sum_own_1))

    got_inner = over_y(given_inner)
    acts = (dense_hidden, acts_y, acts_c, over_c(acts_y))
    sum_inner = sums(inner, gates, inner_goal, 0, F32)
    second = jnp.where(z == 0, weights_l1, weights_r1)
    third = jnp.where(z == 0, weights_l2, jnp.where(z == 3, weights_r2, weights_l1))
    fourth = jnp.where(z == 1, weights_l2, weights_r2)
    sheet = tuple(products(acts, weights, second, third))
    weights_r3, weights_l3, other_a, got_own_1, got_inner, sum_inner, sheet, fourth, own_0, outer_0 = tie(
        (weights_r3, weights_l3, other_a, got_own_1, got_inner, sum_inner, sheet, fourth, own_0, outer_0)
    )

    own_1 = sum_own_1 + got_own_1.astype(F32)
    inner_0 = sum_inner + got_inner.astype(F32)
    (last,) = products(acts, jnp.where(z == 0, weights_l3, jnp.where(z == 3, weights_r3, fourth)))
    s_0, s_1, s_2 = sheet
    of_z = [
        jnp.where(z == 0, s_0, jnp.where(z == 1, s_1, last)),
        jnp.where(z == 1, s_0, jnp.where(z == 3, s_2, s_1)),
        jnp.where(z == 2, s_0, jnp.where(z == 3, s_1, s_2)),
        jnp.where(z == 3, s_0, jnp.where(z == 2, s_2, last)),
    ]
    theirs = jnp.stack([jnp.where(x == 0, of_z[2], of_z[0]), jnp.where(x == 0, of_z[3], of_z[1])]).astype(BF16)
    dense = jnp.stack([jnp.where(x == 0, of_z[0], of_z[2]), jnp.where(x == 0, of_z[1], of_z[3])])
    theirs = lax.ppermute(theirs, "tp", SWAP)
    own_b = jnp.where(z == far, own_1, own_0 + own_a.astype(F32)).astype(BF16)
    other_b = jnp.where(z == 3 - far, inner_0, outer_0 + other_a.astype(F32)).astype(BF16)
    own_b, other_b = tie((own_b, other_b))
    own_b = hop(own_b, [(3, 2), (2, 1)], [(0, 1), (1, 2)])
    other_b = hop(other_b, [(0, 1), (1, 2)], [(3, 2), (2, 1)])
    own_b, other_b, own_1, inner_0 = tie((own_b, other_b, own_1, inner_0))
    dense = dense + theirs.astype(F32)

    own_c = jnp.where(z == far, inner_0, own_b.astype(F32) + jnp.where(distance == 1, own_1, own_0))
    own_c = hop(own_c, left, right)
    other_c = jnp.where(z == 3 - far, own_1, other_b.astype(F32) + jnp.where(distance == 2, inner_0, outer_0))
    other_c = hop(other_c, right, left)
    routed = jnp.where(distance == 3, own_0, jnp.where(distance == 2, own_1, jnp.where(distance == 1, inner_0, outer_0)))
    routed = routed + own_c.astype(F32) + other_c.astype(F32)

    dense = dense.reshape(2, 2, 2, rows, columns)
    near = dense[:, 0, 0]
    by_c = lax.ppermute(dense[:, 1, 0].astype(BF16), "c", SWAP).astype(F32)
    by_y = lax.ppermute(dense[:, 0, 1].astype(BF16), "y", SWAP).astype(F32)
    by_y, far_rows = tie((by_y, dense[:, 1, 1].astype(BF16)))
    by_both = lax.ppermute(far_rows, ("y", "c"), [(0, 3), (1, 2), (2, 1), (3, 0)]).astype(F32)

    def ordered(first, second, swap):
        return jnp.where(swap, second, first), jnp.where(swap, first, second)

    same = jnp.concatenate(ordered(near, by_c, c == 1), 2)
    across = jnp.concatenate(ordered(by_y, by_both, c == 1), 2)
    pair = ordered(same, across, y == 1)
    dense = jnp.concatenate([pair[0][0], pair[1][0], pair[0][1], pair[1][1]], 1)

    zero_gate = jnp.sum(jnp.where(expert_ids < experts, F32(0.0), gate_weights), axis=1)
    identity = zero_gate[:, None] * tokens.astype(F32)
    return (dense + routed + identity).astype(BF16)


def any_mesh(tokens, expert_ids, gate_weights, expert_hidden, expert_down, dense_hidden, dense_down):
    zs, tp = lax.axis_size("z"), lax.axis_size("tp")
    z, y, c, x = (lax.axis_index(name) for name in ("z", "y", "c", "tp"))
    experts = zs * 4
    zt = zs // tp
    rows = tokens.shape[0]
    hidden, down = expert_hidden[0], expert_down[0]
    capacity = hidden.shape[0] // (zt * 4)
    features = down.shape[1]

    hidden = hidden.reshape(zt, 4 * capacity, hidden.shape[1])

    def turn(owner, k):
        return jnp.where(2 * owner < tp, k, zt - 1 - k)

    chunks = []
    for k in range(zt):
        chunks.append((0, k, pick(hidden, turn(x, k))))
    for shift in range(1, tp):
        for k in range(zt):
            sent = chunks[k][2]
            moved = lax.ppermute(sent, "tp", [((i + shift) % tp, i) for i in range(tp)])
            chunks.append((shift, k, moved))

    acts = jnp.stack([dense_hidden, lax.ppermute(dense_hidden, "y", SWAP)])
    acts = acts.reshape(2 * rows, -1)
    columns = dense_down.shape[1]

    def product(weights):
        sibling = lax.ppermute(weights, "c", SWAP)
        first = jnp.where(c == 0, weights, sibling)
        second = jnp.where(c == 0, sibling, weights)
        both = jnp.concatenate([first, second], 1)
        return jnp.dot(acts, both, preferred_element_type=F32).astype(BF16)

    sheet = jnp.zeros((zs, 2 * rows, 2 * columns), BF16)
    every = lax.all_gather(dense_down, "z")
    for i in range(zs):
        sheet = lax.dynamic_update_index_in_dim(sheet, product(every[i]), i, 0)

    gates = spread_gates(gate_rows(expert_ids, gate_weights, experts), zs, y, z)
    high, low = placement(gates, capacity)

    def partial_sum(chunk, at):
        out = jnp.dot(chunk, down, preferred_element_type=F32).astype(BF16)
        out = out.reshape(2, 2, capacity, features)
        sibling = lax.ppermute(pick(out, 1 - c, 1), "c", SWAP)
        table = jnp.concatenate([pick(out, c, 1), sibling], 1)
        p_high, p_low = pick(high, at), pick(low, at)

        def combined(which):
            t = pick(table, which)
            return jnp.dot(pick(p_high, which), t, preferred_element_type=F32) + jnp.dot(
                pick(p_low, which), t, preferred_element_type=F32
            )

        sent = lax.ppermute(combined(1 - y).astype(BF16), "y", SWAP)
        return combined(y) + sent.astype(F32)

    totals = jnp.zeros((zs, rows, features), BF16)
    for shift, k, chunk in chunks:
        owner = (x + shift) % tp
        at = owner * zt + turn(owner, k)
        totals = lax.dynamic_update_index_in_dim(totals, partial_sum(chunk, at).astype(BF16), at, 0)
    routed = lax.psum_scatter(totals, "z", scatter_dimension=0).astype(F32)

    sheet = sheet.reshape(tp, zt, 2 * rows, 2 * columns)
    dense = pick(sheet, x).astype(F32)
    for shift in range(1, tp):
        sent = pick(sheet, (x + shift) % tp)
        dense = dense + lax.ppermute(sent, "tp", [(i, (i + shift) % tp) for i in range(tp)]).astype(F32)
    dense = dense.reshape(zt, 2, rows, 2 * columns)
    theirs = lax.ppermute(dense[:, 1].astype(BF16), "y", SWAP).astype(F32)
    mine = dense[:, 0]
    both = jnp.stack([jnp.where(y == 0, mine, theirs), jnp.where(y == 0, theirs, mine)], 1)
    dense = jnp.moveaxis(both, 2, 0).reshape(rows, features)

    zero_gate = jnp.sum(jnp.where(expert_ids < experts, F32(0.0), gate_weights), axis=1)
    identity = zero_gate[:, None] * tokens.astype(F32)
    return (dense + routed + identity).astype(BF16)


def solution(mesh):
    groups, ranks, tp = mesh.devices.shape
    split = Mesh(mesh.devices.reshape(groups, ranks // 4, 2, 2, tp), ("grp", "z", "y", "c", "tp"))
    ep = ("z", "y", "c")
    return jax.shard_map(
        four_by_two if ranks == 16 and tp == 2 else any_mesh,
        mesh=split,
        in_specs=(
            P(("grp",) + ep, "tp"),
            P(("grp",) + ep, None),
            P(("grp",) + ep, None),
            P(ep, ("grp", "tp"), None),
            P(ep, None, "tp"),
            P(("grp",) + ep, "tp"),
            P("tp", ep),
        ),
        out_specs=P(("grp",) + ep, "tp"),
        check_vma=False,
    )
```
